32 devices in a mesh: dp: 16 (over z, y, core), seq: 2 (over x).
Axes of the slice: x: 2, y: 2, z: 4, core: 2. Of those that a mesh axis runs over, the one named last changes fastest.
Arguments:
- tokens: bfloat16 [64, 1024, 1024], P('dp', 'seq'), may hold values from -6 to 6
- condition: float32 [64, 1024], P('dp'), may hold values from -6 to 6
- w_ada: bfloat16 [1024, 6144], P('dp', 'seq'), may hold values from -0.1875 to 0.1875
- b_ada: bfloat16 [6144], P(('dp', 'seq')), may hold values from -3 to 3
- w_qkv: bfloat16 [1024, 3072], P('dp', 'seq'), may hold values from -0.1875 to 0.1875
- q_bias: bfloat16 [1024], P(('dp', 'seq')), may hold values from -3 to 3
- v_bias: bfloat16 [1024], P(('dp', 'seq')), may hold values from -3 to 3
- w_proj: bfloat16 [1024, 1024], P('dp', 'seq'), may hold values from -0.5 to 0.5
- b_proj: bfloat16 [1024], P(('dp', 'seq')), may hold values from -3 to 3
- w_fc1: bfloat16 [1024, 4096], P('dp', 'seq'), may hold values from -0.1875 to 0.1875
- b_fc1: bfloat16 [4096], P(('dp', 'seq')), may hold values from -3 to 3
- w_fc2: bfloat16 [4096, 1024], P('dp', 'seq'), may hold values from -0.09375 to 0.09375
- b_fc2: bfloat16 [1024], P(('dp', 'seq')), may hold values from -3 to 3
- cotangent: bfloat16 [64, 1024, 1024], P('dp', 'seq'), may hold values from -6 to 6
Outputs:
- output: bfloat16 [64, 1024, 1024], P('dp', 'seq')
- grad_tokens: float32 [64, 1024, 1024], P('dp', 'seq')
- grad_condition: float32 [64, 1024], P('dp')
- grad_w_ada: float32 [1024, 6144], P('dp', 'seq')
- grad_b_ada: float32 [6144], P(('dp', 'seq'))
- grad_w_qkv: float32 [1024, 3072], P('dp', 'seq')
- grad_q_bias: float32 [1024], P(('dp', 'seq'))
- grad_v_bias: float32 [1024], P(('dp', 'seq'))
- grad_w_proj: float32 [1024, 1024], P('dp', 'seq')
- grad_b_proj: float32 [1024], P(('dp', 'seq'))
- grad_w_fc1: float32 [1024, 4096], P('dp', 'seq')
- grad_b_fc1: float32 [4096], P(('dp', 'seq'))
- grad_w_fc2: float32 [4096, 1024], P('dp', 'seq')
- grad_b_fc2: float32 [1024], P(('dp', 'seq'))
The draws below stay inside these ranges and needn't reach their ends.
All inputs are finite; a program needn't handle non-finite values.
Results may differ from the reference program's by a relative error of at most 0.02.
Values may be sent and summed in bfloat16 or wider, within the bound.
No kernel may reach another device: no remote copies, remote signals or barrier semaphores. Data moves between devices by JAX's collectives and lax.ppermute only.
A program may use at most 704 MiB of HBM per device.

```python
import jax
import jax.numpy as jnp
from jax import lax

D = 1024
HEADS = 16
HEAD_DIM = 64
MLP = 4096
SEQ_LEN = 1024
LATENTS = 64


def levels(rng, dims, shards, low, largest):
    level = 1.0
    for position, shards_of in shards:
        steps = jax.random.uniform(jax.random.fold_in(jax.random.fold_in(rng, 6), position), (shards_of,), jnp.float32, low / len(shards), largest / len(shards))
        level = level * jnp.repeat(jnp.exp(steps), dims[position] // shards_of).reshape((-1,) + (1,) * (len(dims) - 1 - position))
    return level


def centred(stream_key, dims, width, reach, cuts=(), kind=jnp.bfloat16):
    values = jax.random.normal(stream_key, dims, jnp.float32) * width
    if len(cuts) > 0:
        values = levels(stream_key, dims, cuts, -0.22, 0.18) * values
    return jnp.clip(values, min=-reach, max=reach).astype(kind)


def setup_inputs(seed: int = 0) -> dict:
    key_of = jax.random.split(jax.random.key(seed), 15)
    tokens = centred(key_of[0], (LATENTS, SEQ_LEN, D), 1.0, 6.0, ((0, 16), (1, 2)))
    condition = centred(key_of[1], (LATENTS, D), 1.0, 6.0, ((0, 16),), jnp.float32)
    w_ada = centred(key_of[2], (D, 6 * D), D ** -0.5, 0.1875, ((0, 16), (1, 2)))
    b_ada = centred(key_of[3], (6 * D,), 0.5, 3.0, ((0, 32),))
    w_qkv = centred(key_of[4], (D, 3 * D), D ** -0.5, 0.1875, ((0, 16), (1, 2)))
    q_bias = centred(key_of[5], (D,), 0.5, 3.0, ((0, 32),))
    v_bias = centred(key_of[6], (D,), 0.5, 3.0, ((0, 32),))
    w_proj = centred(key_of[7], (D, D), (D // 8) ** -0.5, 0.5, ((0, 16), (1, 2)))
    b_proj = centred(key_of[8], (D,), 0.5, 3.0, ((0, 32),))
    w_fc1 = centred(key_of[9], (D, MLP), D ** -0.5, 0.1875, ((0, 16), (1, 2)))
    b_fc1 = centred(key_of[10], (MLP,), 0.5, 3.0, ((0, 32),))
    w_fc2 = centred(key_of[11], (MLP, D), MLP ** -0.5, 0.09375, ((0, 16), (1, 2)))
    b_fc2 = centred(key_of[12], (D,), 0.5, 3.0, ((0, 32),))
    cotangent = centred(key_of[13], (LATENTS, SEQ_LEN, D), 1.0, 6.0, ((0, 16), (1, 2)))
    return {"tokens": tokens, "condition": condition, "w_ada": w_ada, "b_ada": b_ada, "w_qkv": w_qkv, "q_bias": q_bias, "v_bias": v_bias, "w_proj": w_proj, "b_proj": b_proj, "w_fc1": w_fc1, "b_fc1": b_fc1, "w_fc2": w_fc2, "b_fc2": b_fc2, "cotangent": cotangent}


@jax.custom_vjp
def low(v):
    return lax.optimization_barrier(v.astype(jnp.bfloat16)).astype(jnp.float32)

@jax.custom_vjp
def low_back(v):
    return v

def low_keep(v):
    return (low(v), None)

def low_pass(kept, grad):
    return (grad,)

def back_keep(v):
    return (v, None)

def back_low(kept, grad):
    return (low(grad),)
low.defvjp(low_keep, low_pass)
low_back.defvjp(back_keep, back_low)

def both_ways(value):
    return low_back(low(value))

def dense(left, right):
    return jnp.dot(left, right, precision=lax.Precision.HIGHEST)

def normalize(rows):
    centre = rows - lax.optimization_barrier(jnp.mean(rows, axis=-1, keepdims=True))
    return centre * lax.rsqrt(lax.optimization_barrier(jnp.mean(centre * centre, axis=-1, keepdims=True)) + 1e-06)

def latent_block(params, latent_rows, cond_vector):
    w_ada, b_ada, w_qkv, q_bias, v_bias, w_proj, b_proj, w_fc1, b_fc1, w_fc2, b_fc2 = params
    smooth = low(jax.nn.silu(cond_vector))
    modulation = low_back(dense(smooth[None, :], w_ada)[0] + b_ada)
    shift_one, scale_one, gate_one, shift_two, scale_two, gate_two = jnp.split(modulation, 6)
    first_in = low(normalize(latent_rows) * (1.0 + scale_one) + shift_one)
    projected = dense(first_in, w_qkv) + jnp.concatenate([q_bias, jnp.zeros_like(q_bias), v_bias])
    query_rows = both_ways(projected[:, :D]).reshape(SEQ_LEN, HEADS, HEAD_DIM)
    key_rows = both_ways(projected[:, D:2 * D]).reshape(SEQ_LEN, HEADS, HEAD_DIM)
    value_rows = both_ways(projected[:, 2 * D:]).reshape(SEQ_LEN, HEADS, HEAD_DIM)
    scores = low_back(jnp.einsum('qhd,khd->hqk', query_rows, key_rows, precision=lax.Precision.HIGHEST) * HEAD_DIM ** (-0.5))
    softmaxed = jax.nn.softmax(scores, axis=-1)
    attended = jnp.einsum('hqk,khd->qhd', low(softmaxed), value_rows, precision=lax.Precision.HIGHEST)
    attended = both_ways(attended.reshape(SEQ_LEN, D))
    attention = low_back(dense(attended, w_proj) + b_proj)
    middle = latent_rows + gate_one * attention
    second_in = low(normalize(middle) * (1.0 + scale_two) + shift_two)
    hidden = low_back(dense(second_in, w_fc1) + b_fc1)
    active = low(jax.nn.gelu(hidden, approximate=True))
    branch = low_back(dense(active, w_fc2) + b_fc2)
    return middle + gate_two * branch

def forward(all_rows, all_conds, params):

    def one_latent(pair):
        return latent_block(params, pair[0], pair[1])
    return lax.map(jax.checkpoint(one_latent), (all_rows, all_conds))

def reference(tokens, condition, w_ada, b_ada, w_qkv, q_bias, v_bias, w_proj, b_proj, w_fc1, b_fc1, w_fc2, b_fc2, cotangent):
    params = tuple((item.astype(jnp.float32) for item in (w_ada, b_ada, w_qkv, q_bias, v_bias, w_proj, b_proj, w_fc1, b_fc1, w_fc2, b_fc2)))
    result, pull = jax.vjp(forward, tokens.astype(jnp.float32), condition.astype(jnp.float32), params)
    grad_rows, grad_cond, grad_params = pull(cotangent.astype(jnp.float32))
    return (result.astype(jnp.bfloat16), grad_rows, grad_cond, grad_params[0], grad_params[1], grad_params[2], grad_params[3], grad_params[4], grad_params[5], grad_params[6], grad_params[7], grad_params[8], grad_params[9], grad_params[10])
```

```python
import functools

import jax
import jax.numpy as jnp
from jax import lax
from jax.experimental import pallas as pl
from jax.experimental.pallas import tpu as pltpu
from jax.sharding import PartitionSpec as P

HEADS = 16
LOW = jnp.bfloat16
WIDE = jnp.float32
LOG2E = 1.4426950408889634


def normalize(rows):
    centre = rows - jnp.mean(rows, axis=-1, keepdims=True)
    return centre * lax.rsqrt(jnp.mean(centre * centre, axis=-1, keepdims=True) + 1e-06)


def gelu_tanh(value):
    return jax.nn.gelu(value, approximate=True)


def matmul(left, right):
    return jnp.dot(left, right, preferred_element_type=jnp.float32)


def contract_rows(left, right):
    return lax.dot_general(
        left, right, (((0,), (0,)), ((), ())), preferred_element_type=jnp.float32
    )


def contract_cols(left, right):
    return lax.dot_general(
        left, right, (((1,), (1,)), ((), ())), preferred_element_type=jnp.float32
    )


def collect_fore(w_ada, w_qkv, w_proj, w_fc1, w_fc2, b_ada, q_bias, v_bias, b_proj, b_fc1, b_fc2):
    inner = (
        lax.all_gather(w_ada, "seq", axis=1, tiled=True),
        lax.all_gather(w_qkv, "seq", axis=1, tiled=True),
        lax.all_gather(w_proj, "seq", axis=1, tiled=True),
        lax.all_gather(w_fc1, "seq", axis=1, tiled=True),
        lax.all_gather(w_fc2, "seq", axis=1, tiled=True),
        lax.all_gather(b_ada, "seq", axis=0, tiled=True),
        lax.all_gather(q_bias, "seq", axis=0, tiled=True),
        lax.all_gather(v_bias, "seq", axis=0, tiled=True),
        lax.all_gather(b_proj, "seq", axis=0, tiled=True),
        lax.all_gather(b_fc1, "seq", axis=0, tiled=True),
        lax.all_gather(b_fc2, "seq", axis=0, tiled=True),
    )
    return (
        lax.all_gather(inner[0], "dp", axis=0, tiled=True),
        lax.all_gather(inner[1], "dp", axis=0, tiled=True),
        lax.all_gather(inner[2], "dp", axis=0, tiled=True),
        lax.all_gather(inner[3], "dp", axis=0, tiled=True),
        lax.all_gather(inner[4], "dp", axis=0, tiled=True),
        lax.all_gather(inner[5], "dp", axis=0, tiled=True),
        lax.all_gather(inner[6], "dp", axis=0, tiled=True),
        lax.all_gather(inner[7], "dp", axis=0, tiled=True),
        lax.all_gather(inner[8], "dp", axis=0, tiled=True),
        lax.all_gather(inner[9], "dp", axis=0, tiled=True),
        lax.all_gather(inner[10], "dp", axis=0, tiled=True),
    )


def collect_back(w_ada, w_qkv, w_proj, w_fc1, w_fc2):
    inner = (
        lax.all_gather(w_ada, "seq", axis=1, tiled=True),
        lax.all_gather(w_qkv, "seq", axis=1, tiled=True),
        lax.all_gather(w_proj, "seq", axis=1, tiled=True),
        lax.all_gather(w_fc1, "seq", axis=1, tiled=True),
        lax.all_gather(w_fc2, "seq", axis=1, tiled=True),
    )
    return (
        lax.all_gather(inner[0], "dp", axis=0, tiled=True),
        lax.all_gather(inner[1], "dp", axis=0, tiled=True),
        lax.all_gather(inner[2], "dp", axis=0, tiled=True),
        lax.all_gather(inner[3], "dp", axis=0, tiled=True),
        lax.all_gather(inner[4], "dp", axis=0, tiled=True),
    )


def general_body(
    tokens,
    condition,
    w_ada,
    b_ada,
    w_qkv,
    q_bias,
    v_bias,
    w_proj,
    b_proj,
    w_fc1,
    b_fc1,
    w_fc2,
    b_fc2,
    cotangent,
):
    latents_here, tokens_here, model_width = tokens.shape
    head_count = HEADS
    head_size = model_width // head_count
    score_scale = head_size ** (-0.5)
    row_count = latents_here * tokens_here
    gathered = collect_fore(
        w_ada, w_qkv, w_proj, w_fc1, w_fc2, b_ada, q_bias, v_bias, b_proj, b_fc1, b_fc2
    )
    full_ada, full_qkv, full_proj, full_fc1, full_fc2 = (
        gathered[0],
        gathered[1],
        gathered[2],
        gathered[3],
        gathered[4],
    )
    bias_ada = gathered[5].astype(jnp.float32)
    bias_query = gathered[6].astype(jnp.float32)
    bias_value = gathered[7].astype(jnp.float32)
    bias_proj = gathered[8].astype(jnp.float32)
    bias_fc1 = gathered[9].astype(jnp.float32)
    bias_fc2 = gathered[10].astype(jnp.float32)
    inputs = tokens.astype(jnp.float32)
    smooth, silu_pull = jax.vjp(jax.nn.silu, condition)
    smooth_low = smooth.astype(jnp.bfloat16)
    mods = matmul(smooth_low, full_ada) + bias_ada
    pieces = [mods[:, None, index * model_width : (index + 1) * model_width] for index in range(6)]
    shift_one, scale_one, gate_one, shift_two, scale_two, gate_two = pieces
    normed_one, norm_pull_one = jax.vjp(normalize, inputs)
    first_rows = (
        (normed_one * (1.0 + scale_one) + shift_one)
        .astype(jnp.bfloat16)
        .reshape(row_count, model_width)
    )
    bias_row = jnp.concatenate([bias_query, jnp.zeros_like(bias_query), bias_value])
    projected = matmul(first_rows, full_qkv) + bias_row
    query = (
        projected[:, :model_width]
        .astype(jnp.bfloat16)
        .reshape(latents_here, tokens_here, head_count, head_size)
    )
    key_local = (
        projected[:, model_width : 2 * model_width]
        .astype(jnp.bfloat16)
        .reshape(latents_here, tokens_here, model_width)
    )
    value_local = (
        projected[:, 2 * model_width :]
        .astype(jnp.bfloat16)
        .reshape(latents_here, tokens_here, model_width)
    )
    key_all, value_all = (
        lax.all_gather(key_local, "seq", axis=1, tiled=True),
        lax.all_gather(value_local, "seq", axis=1, tiled=True),
    )
    key_count = key_all.shape[1]
    key_heads = key_all.reshape(latents_here, key_count, head_count, head_size)
    value_heads = value_all.reshape(latents_here, key_count, head_count, head_size)
    scores = (
        jnp.einsum("bqhd,bkhd->bhqk", query, key_heads, preferred_element_type=jnp.float32)
        * score_scale
    )
    peak = jnp.max(scores, axis=-1, keepdims=True)
    log_total = jnp.log(jnp.sum(jnp.exp(scores - peak), axis=-1, keepdims=True)) + peak
    softmaxed = jnp.exp(scores - log_total)
    attended = jnp.einsum(
        "bhqk,bkhd->bqhd",
        softmaxed.astype(jnp.bfloat16),
        value_heads,
        preferred_element_type=jnp.float32,
    )
    attended = attended.astype(jnp.bfloat16).reshape(row_count, model_width)
    attention = (matmul(attended, full_proj) + bias_proj).reshape(
        latents_here, tokens_here, model_width
    )
    middle = inputs + gate_one * attention
    normed_two, norm_pull_two = jax.vjp(normalize, middle)
    second_rows = (
        (normed_two * (1.0 + scale_two) + shift_two)
        .astype(jnp.bfloat16)
        .reshape(row_count, model_width)
    )
    hidden = matmul(second_rows, full_fc1) + bias_fc1
    active, gelu_pull = jax.vjp(gelu_tanh, hidden)
    active_low = active.astype(jnp.bfloat16)
    branch = (matmul(active_low, full_fc2) + bias_fc2).reshape(
        latents_here, tokens_here, model_width
    )
    output = (middle + gate_two * branch).astype(jnp.bfloat16)
    regained = collect_back(w_ada, w_qkv, w_proj, w_fc1, w_fc2)
    full_ada, full_qkv, full_proj, full_fc1, full_fc2 = (
        regained[0],
        regained[1],
        regained[2],
        regained[3],
        regained[4],
    )
    grad_out = cotangent.astype(jnp.float32)
    gate_two_grad = jnp.sum(grad_out * branch, axis=1)
    branch_grad = (gate_two * grad_out).astype(jnp.bfloat16).reshape(row_count, model_width)
    fc2_bias_grad = jnp.sum(branch_grad.astype(jnp.float32), axis=0)
    fc2_grad = contract_rows(active_low, branch_grad)
    active_grad = contract_cols(branch_grad, full_fc2)
    hidden_grad = gelu_pull(active_grad)[0].astype(jnp.bfloat16)
    fc1_bias_grad = jnp.sum(hidden_grad.astype(jnp.float32), axis=0)
    fc1_grad = contract_rows(second_rows, hidden_grad)
    second_grad = contract_cols(hidden_grad, full_fc1).reshape(
        latents_here, tokens_here, model_width
    )
    shift_two_grad = jnp.sum(second_grad, axis=1)
    scale_two_grad = jnp.sum(second_grad * normed_two, axis=1)
    middle_grad = grad_out + norm_pull_two(second_grad * (1.0 + scale_two))[0]
    gate_one_grad = jnp.sum(middle_grad * attention, axis=1)
    attention_grad = (gate_one * middle_grad).astype(jnp.bfloat16).reshape(row_count, model_width)
    proj_bias_grad = jnp.sum(attention_grad.astype(jnp.float32), axis=0)
    proj_grad = contract_rows(attended, attention_grad)
    attended_grad = contract_cols(attention_grad, full_proj).astype(jnp.bfloat16)
    attended_grad = attended_grad.reshape(latents_here, tokens_here, head_count, head_size)
    scores = (
        jnp.einsum("bqhd,bkhd->bhqk", query, key_heads, preferred_element_type=jnp.float32)
        * score_scale
    )
    softmaxed = jnp.exp(scores - log_total)
    weight_grad = jnp.einsum(
        "bqhd,bkhd->bhqk", attended_grad, value_heads, preferred_element_type=jnp.float32
    )
    row_delta = jnp.sum(softmaxed * weight_grad, axis=-1, keepdims=True)
    score_grad = (softmaxed * (weight_grad - row_delta)).astype(jnp.bfloat16)
    query_grad = (
        jnp.einsum("bhqk,bkhd->bqhd", score_grad, key_heads, preferred_element_type=jnp.float32)
        * score_scale
    )
    key_grad = (
        jnp.einsum("bhqk,bqhd->bkhd", score_grad, query, preferred_element_type=jnp.float32)
        * score_scale
    )
    value_grad = jnp.einsum(
        "bhqk,bqhd->bkhd",
        softmaxed.astype(jnp.bfloat16),
        attended_grad,
        preferred_element_type=jnp.float32,
    )
    key_mine, value_mine = (
        lax.psum_scatter(
            key_grad.reshape(latents_here, key_count, model_width).astype(jnp.bfloat16),
            "seq",
            scatter_dimension=1,
            tiled=True,
        ).astype(jnp.float32),
        lax.psum_scatter(
            value_grad.reshape(latents_here, key_count, model_width).astype(jnp.bfloat16),
            "seq",
            scatter_dimension=1,
            tiled=True,
        ).astype(jnp.float32),
    )
    query_low = query_grad.astype(jnp.bfloat16).reshape(row_count, model_width)
    value_low = value_mine.astype(jnp.bfloat16).reshape(row_count, model_width)
    joint_grad = jnp.concatenate(
        [query_low, key_mine.astype(jnp.bfloat16).reshape(row_count, model_width), value_low],
        axis=-1,
    )
    query_bias_grad = jnp.sum(query_low.astype(jnp.float32), axis=0)
    value_bias_grad = jnp.sum(value_low.astype(jnp.float32), axis=0)
    qkv_grad = contract_rows(first_rows, joint_grad)
    first_grad = contract_cols(joint_grad, full_qkv).reshape(latents_here, tokens_here, model_width)
    shift_one_grad = jnp.sum(first_grad, axis=1)
    scale_one_grad = jnp.sum(first_grad * normed_one, axis=1)
    input_grad = middle_grad + norm_pull_one(first_grad * (1.0 + scale_one))[0]
    mods_grad = jnp.concatenate(
        [
            shift_one_grad,
            scale_one_grad,
            gate_one_grad,
            shift_two_grad,
            scale_two_grad,
            gate_two_grad,
        ],
        axis=-1,
    )
    mods_low = lax.psum(mods_grad.astype(jnp.bfloat16), "seq")
    leader = (lax.axis_index("seq") == 0).astype(jnp.float32)
    ada_grad = contract_rows(smooth_low, mods_low) * leader
    ada_bias_grad = jnp.sum(mods_low.astype(jnp.float32), axis=0) * leader
    smooth_grad = contract_cols(mods_low, full_ada)
    condition_grad = silu_pull(smooth_grad)[0]
    summed = (
        lax.psum_scatter(
            ada_grad.astype(jnp.bfloat16), "dp", scatter_dimension=0, tiled=True
        ).astype(jnp.float32),
        lax.psum_scatter(
            qkv_grad.astype(jnp.bfloat16), "dp", scatter_dimension=0, tiled=True
        ).astype(jnp.float32),
        lax.psum_scatter(
            proj_grad.astype(jnp.bfloat16), "dp", scatter_dimension=0, tiled=True
        ).astype(jnp.float32),
        lax.psum_scatter(
            fc1_grad.astype(jnp.bfloat16), "dp", scatter_dimension=0, tiled=True
        ).astype(jnp.float32),
        lax.psum_scatter(
            fc2_grad.astype(jnp.bfloat16), "dp", scatter_dimension=0, tiled=True
        ).astype(jnp.float32),
        lax.psum_scatter(
            ada_bias_grad.astype(jnp.bfloat16), "dp", scatter_dimension=0, tiled=True
        ).astype(jnp.float32),
        lax.psum_scatter(
            query_bias_grad.astype(jnp.bfloat16), "dp", scatter_dimension=0, tiled=True
        ).astype(jnp.float32),
        lax.psum_scatter(
            value_bias_grad.astype(jnp.bfloat16), "dp", scatter_dimension=0, tiled=True
        ).astype(jnp.float32),
        lax.psum_scatter(
            proj_bias_grad.astype(jnp.bfloat16), "dp", scatter_dimension=0, tiled=True
        ).astype(jnp.float32),
        lax.psum_scatter(
            fc1_bias_grad.astype(jnp.bfloat16), "dp", scatter_dimension=0, tiled=True
        ).astype(jnp.float32),
        lax.psum_scatter(
            fc2_bias_grad.astype(jnp.bfloat16), "dp", scatter_dimension=0, tiled=True
        ).astype(jnp.float32),
    )
    owned = (
        lax.psum_scatter(
            summed[0].astype(jnp.bfloat16), "seq", scatter_dimension=1, tiled=True
        ).astype(jnp.float32),
        lax.psum_scatter(
            summed[1].astype(jnp.bfloat16), "seq", scatter_dimension=1, tiled=True
        ).astype(jnp.float32),
        lax.psum_scatter(
            summed[2].astype(jnp.bfloat16), "seq", scatter_dimension=1, tiled=True
        ).astype(jnp.float32),
        lax.psum_scatter(
            summed[3].astype(jnp.bfloat16), "seq", scatter_dimension=1, tiled=True
        ).astype(jnp.float32),
        lax.psum_scatter(
            summed[4].astype(jnp.bfloat16), "seq", scatter_dimension=1, tiled=True
        ).astype(jnp.float32),
        lax.psum_scatter(
            summed[5].astype(jnp.bfloat16), "seq", scatter_dimension=0, tiled=True
        ).astype(jnp.float32),
        lax.psum_scatter(
            summed[6].astype(jnp.bfloat16), "seq", scatter_dimension=0, tiled=True
        ).astype(jnp.float32),
        lax.psum_scatter(
            summed[7].astype(jnp.bfloat16), "seq", scatter_dimension=0, tiled=True
        ).astype(jnp.float32),
        lax.psum_scatter(
            summed[8].astype(jnp.bfloat16), "seq", scatter_dimension=0, tiled=True
        ).astype(jnp.float32),
        lax.psum_scatter(
            summed[9].astype(jnp.bfloat16), "seq", scatter_dimension=0, tiled=True
        ).astype(jnp.float32),
        lax.psum_scatter(
            summed[10].astype(jnp.bfloat16), "seq", scatter_dimension=0, tiled=True
        ).astype(jnp.float32),
    )
    return (
        output,
        input_grad,
        condition_grad,
        owned[0],
        owned[5],
        owned[1],
        owned[6],
        owned[7],
        owned[2],
        owned[8],
        owned[3],
        owned[9],
        owned[4],
        owned[10],
    )


NT = (((1,), (1,)), ((), ()))
NN = (((1,), (0,)), ((), ()))


def product(left, right, dims):
    return lax.dot_general(left, right, dims, preferred_element_type=WIDE)


def flat(ref):
    value = ref[...]
    return value.reshape(value.shape[0] * value.shape[2], value.shape[3])


def attention_kernel(q_ref, k_ref, v_ref, o_ref, e_ref, r_ref, *, size, chunk):
    q, k, v = flat(q_ref), flat(k_ref), flat(v_ref)
    count = q.shape[0]
    scaled = q.astype(WIDE) * (LOG2E * size**-0.5)
    high = scaled.astype(LOW)
    rest = (scaled - high.astype(WIDE)).astype(LOW)
    v_t = v.astype(WIDE).T.astype(LOW)
    ones = jnp.ones((16, count), LOW)
    outs, inverses = [], []
    for head in range(q.shape[1] // size):
        cols = slice(head * size, (head + 1) * size)
        keys = jnp.concatenate([k[:, cols], k[:, cols]], 1)
        queries = jnp.concatenate([high[:, cols], rest[:, cols]], 1)
        values = jnp.concatenate([v_t[cols], ones], 0)
        out_parts, inverse_parts = [], []
        for at in range(0, count, chunk):
            scores = product(keys, queries[at : at + chunk], NT)
            peak = jnp.max(scores, axis=0, keepdims=True)
            weights = jnp.exp2(scores - peak).astype(LOW)
            e_ref[0, 0, head, :, at : at + chunk] = weights
            summed = product(values, weights, NN)
            inverse = 1.0 / summed[size : size + 1]
            out_parts.append(summed[:size] * inverse)
            inverse_parts.append(inverse)
        outs.append(jnp.concatenate(out_parts, 1))
        inverses.append(jnp.concatenate(inverse_parts, 1))
    o_ref[...] = jnp.concatenate(outs, 0).T.astype(LOW).reshape(o_ref.shape)
    r_ref[0, 0] = jnp.concatenate(inverses, 0)


def attention_back_kernel(
    q_ref, k_ref, v_ref, o_ref, do_ref, e_ref, r_ref, dq_ref, dk_ref, dv_ref, *, size
):
    q, k, v = flat(q_ref), flat(k_ref), flat(v_ref)
    do, o = flat(do_ref).astype(WIDE), flat(o_ref).astype(WIDE)
    scale = size**-0.5
    inverse = r_ref[0, 0]
    prod_t = (do * o).T
    do_t = do.T
    k_t = (k.astype(WIDE) * scale).T.astype(LOW)
    q_scaled = (q.astype(WIDE) * scale).astype(LOW)
    dqs, dks, dvs = [], [], []
    for head in range(q.shape[1] // size):
        cols = slice(head * size, (head + 1) * size)
        inv = inverse[head : head + 1]
        grad_t = do_t[cols] * inv
        delta = jnp.sum(prod_t[cols], axis=0, keepdims=True) * inv
        weights = e_ref[0, 0, head]
        da = product(v[:, cols], grad_t.astype(LOW), NN)
        ds = weights * (da - delta).astype(LOW)
        dqs.append(product(k_t[cols], ds, NN))
        dks.append(product(ds, q_scaled[:, cols], NN))
        dvs.append(product(weights, grad_t.T.astype(LOW), NN))
    dq_ref[...] = jnp.concatenate(dqs, 0).T.astype(LOW).reshape(dq_ref.shape)
    dk_ref[...] = jnp.concatenate(dks, 1).astype(LOW).reshape(dk_ref.shape)
    dv_ref[...] = jnp.concatenate(dvs, 1).astype(LOW).reshape(dv_ref.shape)


PARAMS = pltpu.CompilerParams(vmem_limit_bytes=56 << 20)


def attention_blocks(half, tokens, width):
    def columns(base):
        return pl.BlockSpec((half, 1, tokens, width), lambda latent, pair: (0, latent, 0, base + pair))

    return columns


def attention_fore(qkv):
    half, latents, tokens, triple = qkv.shape
    model = triple // 3
    size = model // HEADS
    per = 128 // size
    pairs = HEADS // per
    count = half * tokens
    columns = attention_blocks(half, tokens, 128)
    flops = 4 * latents * HEADS * count * count * 128
    return pl.pallas_call(
        functools.partial(attention_kernel, size=size, chunk=count),
        grid=(latents, pairs),
        in_specs=[columns(0), columns(pairs), columns(2 * pairs)],
        out_specs=[
            columns(0),
            pl.BlockSpec((1, 1, per, count, count), lambda latent, pair: (latent, pair, 0, 0, 0)),
            pl.BlockSpec((1, 1, per, count), lambda latent, pair: (latent, pair, 0, 0)),
        ],
        out_shape=[
            jax.ShapeDtypeStruct((half, latents, tokens, model), LOW),
            jax.ShapeDtypeStruct((latents, pairs, per, count, count), LOW),
            jax.ShapeDtypeStruct((latents, pairs, per, count), WIDE),
        ],
        compiler_params=PARAMS,
        cost_estimate=pl.CostEstimate(
            flops=flops, bytes_accessed=90 << 20, transcendentals=latents * HEADS * count * count
        ),
        name="attention_fore",
    )(qkv, qkv, qkv)


def attention_back(qkv, attended, attended_grad, weights, inverse):
    half, latents, tokens, triple = qkv.shape
    model = triple // 3
    size = model // HEADS
    per = 128 // size
    pairs = HEADS // per
    count = half * tokens
    columns = attention_blocks(half, tokens, 128)
    flops = 8 * latents * HEADS * count * count * 128
    grads = jax.ShapeDtypeStruct((half, latents, tokens, model), LOW)
    return pl.pallas_call(
        functools.partial(attention_back_kernel, size=size),
        grid=(latents, pairs),
        in_specs=[
            columns(0),
            columns(pairs),
            columns(2 * pairs),
            columns(0),
            columns(0),
            pl.BlockSpec((1, 1, per, count, count), lambda latent, pair: (latent, pair, 0, 0, 0)),
            pl.BlockSpec((1, 1, per, count), lambda latent, pair: (latent, pair, 0, 0)),
        ],
        out_specs=[columns(0)] * 3,
        out_shape=[grads] * 3,
        compiler_params=PARAMS,
        cost_estimate=pl.CostEstimate(flops=flops, bytes_accessed=100 << 20, transcendentals=0),
        name="attention_back",
    )(qkv, qkv, qkv, attended, attended_grad, weights, inverse)


class Wires:
    def __init__(self, dp):
        self.depth = dp // 4
        index = lax.axis_index("dp")
        self.z, self.y, self.core = index // 4, (index // 2) % 2, index % 2
        self.x = lax.axis_index("seq")
        self.places = [(z, y, c) for z in range(self.depth) for y in range(2) for c in range(2)]

    def across(self, value):
        return lax.ppermute(value, "seq", [(0, 1), (1, 0)])

    def dp_step(self, value, move):
        pairs = []
        for z, y, c in self.places:
            to_z, to_y, to_c = move(z, y, c)
            pairs.append(((z * 2 + y) * 2 + c, (to_z * 2 + to_y) * 2 + to_c))
        return lax.ppermute(value, "dp", pairs)

    def distances(self):
        steps, distance = [], self.depth // 2
        while distance:
            steps.append(distance)
            distance //= 2
        return steps

    def bit(self, distance):
        return (self.z // distance) % 2

    def mirror(self, value, distance):
        return self.dp_step(value, lambda z, y, c: (z ^ distance, y, c))

    def beside(self, value):
        return self.dp_step(value, lambda z, y, c: (z, 1 - y, c))

    def twin(self, value):
        return self.dp_step(value, lambda z, y, c: (z, y, 1 - c))


def pick(value, index, axis):
    return lax.dynamic_index_in_dim(value, index, axis, keepdims=False)


def order_two(mine, other, index, axis, fresh=False):
    if fresh:
        mine, other = mine[:, None], other[:, None]
        both = order_two(mine, other, index, 1)
        return both.reshape((-1,) + both.shape[2:])
    return jnp.where(
        index == 0,
        jnp.concatenate([mine, other], axis),
        jnp.concatenate([other, mine], axis),
    )


def gather_small(wires, value):
    held = value[None]
    for distance in wires.distances():
        held = order_two(held, wires.mirror(held, distance), wires.bit(distance), 0, True)
    held = order_two(held, wires.beside(held), wires.y, 0, True)
    held = order_two(held, wires.twin(held), wires.core, 0, True)
    return held


def sum_small(wires, value):
    held = value.reshape((wires.depth, 2, 2) + value.shape[1:])
    held = pick(held, wires.core, 2) + wires.twin(pick(held, 1 - wires.core, 2))
    held = pick(held, wires.y, 1) + wires.beside(pick(held, 1 - wires.y, 1))
    distances = wires.distances()
    held = held.reshape((2,) * len(distances) + held.shape[1:])
    for place, distance in reversed(list(enumerate(distances))):
        bit = wires.bit(distance)
        held = pick(held, bit, place) + wires.mirror(pick(held, 1 - bit, place), distance)
    return held


def gather_weight(shard):
    return lax.all_gather(shard, "dp", axis=0, tiled=True)


def scatter_grad(wires, grad):
    held = lax.psum_scatter(grad, "dp", scatter_dimension=0, tiled=True)
    halves = held.reshape(held.shape[0], 2, held.shape[1] // 2)
    theirs = wires.across(pick(halves, 1 - wires.x, 1))
    return pick(halves, wires.x, 1).astype(WIDE) + theirs.astype(WIDE)


def fast_body(
    dp,
    tokens,
    condition,
    w_ada,
    b_ada,
    w_qkv,
    q_bias,
    v_bias,
    w_proj,
    b_proj,
    w_fc1,
    b_fc1,
    w_fc2,
    b_fc2,
    cotangent,
):
    wires = Wires(dp)
    group, tokens_here, model = tokens.shape
    mine = group // 2
    rows = group * tokens_here
    x, z_y_c = wires.x, lax.axis_index("dp")

    def swap(value):
        ours = lax.dynamic_slice_in_dim(value, x * mine, mine, 0)
        theirs = lax.dynamic_slice_in_dim(value, (1 - x) * mine, mine, 0)
        return ours, wires.across(theirs)

    def swap_back(value, kind):
        ours, theirs = value[0].astype(kind), wires.across(value[1].astype(LOW)).astype(kind)
        return order_two(ours, theirs, x, 0)

    packed = jnp.concatenate([w_qkv, w_proj, w_fc1], axis=1)
    theirs = wires.across(packed)
    cuts = [w_qkv.shape[1], w_qkv.shape[1] + w_proj.shape[1]]
    own_qkv, own_proj, own_fc1 = (
        order_two(a, b, x, 1) for a, b in zip(jnp.split(packed, cuts, 1), jnp.split(theirs, cuts, 1))
    )
    own_fc2 = order_two(w_fc2, wires.across(w_fc2), x, 1)
    full_qkv = gather_weight(own_qkv)
    full_both = gather_weight(jnp.concatenate([own_proj, own_fc1], axis=1))
    full_proj, full_fc1 = full_both[:, :model], full_both[:, model:]
    full_fc2 = gather_weight(own_fc2)
    tokens_two = jnp.stack(swap(tokens))
    cotangent_two = jnp.stack(swap(cotangent))

    vectors = (q_bias, v_bias, b_proj, b_fc1, b_fc2, b_ada)
    sizes = [v.shape[0] for v in vectors]
    offsets = [sum(sizes[:i]) for i in range(len(sizes))]
    biases = jnp.concatenate(vectors)[None]
    biases = order_two(biases, wires.across(biases), x, 0)
    smooth, silu_pull = jax.vjp(jax.nn.silu, condition)
    smooth_low = smooth.astype(LOW)
    vector = jnp.concatenate([smooth_low.reshape(-1), biases.reshape(-1)])
    vector = gather_small(wires, vector)
    joined = vector[:, group * model :].reshape(2 * dp, -1)
    bias_query, bias_value, bias_proj, bias_fc1, bias_fc2, bias_ada = (
        joined[:, o : o + n].reshape(-1).astype(WIDE) for o, n in zip(offsets, sizes)
    )

    smooth_all = vector[:, : group * model].reshape(dp * group, model)
    ada_rows = w_ada.shape[0]
    smooth_mine = lax.dynamic_slice_in_dim(smooth_all, z_y_c * ada_rows, ada_rows, 1)
    partial = matmul(smooth_mine, w_ada)
    half_mods = sum_small(wires, partial.reshape(dp, group, -1))
    ours, theirs = swap(half_mods)
    mods = order_two(ours, theirs, x, 1) + bias_ada
    pieces = [mods[None, :, None, i * model : (i + 1) * model] for i in range(6)]
    shift_one, scale_one, gate_one, shift_two, scale_two, gate_two = pieces
    four = (2, mine, tokens_here, model)

    inputs = tokens_two.astype(WIDE)
    normed_one, norm_pull_one = jax.vjp(normalize, inputs)
    first_rows = (normed_one * (1.0 + scale_one) + shift_one).astype(LOW).reshape(rows, model)
    bias_row = jnp.concatenate([bias_query, jnp.zeros_like(bias_query), bias_value])
    qkv = (matmul(first_rows, full_qkv) + bias_row).astype(LOW)
    qkv = qkv.reshape(2, mine, tokens_here, 3 * model)
    attended, weights, inverse = attention_fore(qkv)
    attended_rows = attended.reshape(rows, model)
    attention = (matmul(attended_rows, full_proj) + bias_proj).reshape(four)
    middle = inputs + gate_one * attention
    normed_two, norm_pull_two = jax.vjp(normalize, middle)
    second_rows = (normed_two * (1.0 + scale_two) + shift_two).astype(LOW).reshape(rows, model)
    hidden = matmul(second_rows, full_fc1) + bias_fc1
    active, gelu_pull = jax.vjp(gelu_tanh, hidden)
    active_low = active.astype(LOW)
    branch = (matmul(active_low, full_fc2) + bias_fc2).reshape(four)
    output = swap_back((middle + gate_two * branch).astype(LOW), LOW)

    grad_out = cotangent_two.astype(WIDE)
    gate_two_grad = jnp.sum(grad_out * branch, axis=(0, 2))
    branch_grad = (gate_two * grad_out).astype(LOW).reshape(rows, model)
    fc2_bias_grad = jnp.sum(branch_grad.astype(WIDE), axis=0)
    fc2_grad = scatter_grad(wires, contract_rows(active_low, branch_grad).astype(LOW))
    active_grad = contract_cols(branch_grad, full_fc2)
    hidden_grad = gelu_pull(active_grad)[0].astype(LOW)
    fc1_bias_grad = jnp.sum(hidden_grad.astype(WIDE), axis=0)
    fc1_grad = scatter_grad(wires, contract_rows(second_rows, hidden_grad).astype(LOW))
    second_grad = contract_cols(hidden_grad, full_fc1).reshape(four)
    shift_two_grad = jnp.sum(second_grad, axis=(0, 2))
    scale_two_grad = jnp.sum(second_grad * normed_two, axis=(0, 2))
    middle_grad = grad_out + norm_pull_two(second_grad * (1.0 + scale_two))[0]
    gate_one_grad = jnp.sum(middle_grad * attention, axis=(0, 2))
    attention_grad = (gate_one * middle_grad).astype(LOW).reshape(rows, model)
    proj_bias_grad = jnp.sum(attention_grad.astype(WIDE), axis=0)
    proj_grad = scatter_grad(wires, contract_rows(attended_rows, attention_grad).astype(LOW))
    attended_grad = contract_cols(attention_grad, full_proj).astype(LOW).reshape(four)
    dq, dk, dv = attention_back(qkv, attended, attended_grad, weights, inverse)
    joint = jnp.concatenate([d.reshape(rows, model) for d in (dq, dk, dv)], axis=-1)
    query_bias_grad = jnp.sum(dq.astype(WIDE), axis=(0, 1, 2))
    value_bias_grad = jnp.sum(dv.astype(WIDE), axis=(0, 1, 2))
    qkv_grad = scatter_grad(wires, contract_rows(first_rows, joint).astype(LOW))
    first_grad = contract_cols(joint, full_qkv).reshape(four)
    shift_one_grad = jnp.sum(first_grad, axis=(0, 2))
    scale_one_grad = jnp.sum(first_grad * normed_one, axis=(0, 2))
    input_grad = swap_back(middle_grad + norm_pull_one(first_grad * (1.0 + scale_one))[0], WIDE)

    mods_grad = jnp.concatenate(
        [shift_one_grad, scale_one_grad, gate_one_grad, shift_two_grad, scale_two_grad, gate_two_grad],
        axis=-1,
    ).astype(LOW)
    halves = mods_grad.reshape(mine, 2, 3 * model)
    group_grad = order_two(
        pick(halves, x, 1), wires.across(pick(halves, 1 - x, 1)), x, 0
    )
    all_grad = gather_small(wires, group_grad).reshape(dp * group, -1)
    ada_grad = contract_rows(smooth_mine, all_grad)
    half_sum = jnp.sum(all_grad.astype(WIDE), axis=0)
    both_sums = order_two(half_sum, wires.across(half_sum), x, 0)
    ada_bias_grad = lax.dynamic_slice_in_dim(
        both_sums, (z_y_c * 2 + x) * b_ada.shape[0], b_ada.shape[0], 0
    )
    smooth_part = contract_cols(all_grad, w_ada)
    smooth_part = smooth_part + wires.across(smooth_part)
    sums = (query_bias_grad, value_bias_grad, proj_bias_grad, fc1_bias_grad, fc2_bias_grad)
    bias_sums = jnp.concatenate([v.reshape(2 * dp, -1) for v in sums], axis=1).reshape(dp, 2, -1)
    bias_sums = sum_small(wires, bias_sums)
    owned = pick(bias_sums, x, 0) + wires.across(pick(bias_sums, 1 - x, 0))
    spread = lax.all_to_all(
        smooth_part.reshape(dp, group, ada_rows), "dp", 0, 0, tiled=False
    )
    smooth_grad = jnp.swapaxes(spread, 0, 1).reshape(group, model)
    condition_grad = silu_pull(smooth_grad)[0]

    bias_grads = [owned[o : o + n] for o, n in zip(offsets, sizes[:5])]
    return (
        output,
        input_grad,
        condition_grad,
        ada_grad,
        ada_bias_grad,
        qkv_grad,
        bias_grads[0],
        bias_grads[1],
        proj_grad,
        bias_grads[2],
        fc1_grad,
        bias_grads[3],
        fc2_grad,
        bias_grads[4],
    )


def solution(mesh):
    sizes = dict(mesh.shape)

    def body(tokens, *others):
        split = sizes["seq"] == 2 and sizes["dp"] % 4 == 0 and tokens.shape[0] % 2 == 0
        if split:
            return fast_body(sizes["dp"], tokens, *others)
        return general_body(tokens, *others)

    return jax.shard_map(
        body,
        mesh=mesh,
        in_specs=(
            P("dp", "seq", None),
            P("dp", None),
            P("dp", "seq"),
            P(("dp", "seq")),
            P("dp", "seq"),
            P(("dp", "seq")),
            P(("dp", "seq")),
            P("dp", "seq"),
            P(("dp", "seq")),
            P("dp", "seq"),
            P(("dp", "seq")),
            P("dp", "seq"),
            P(("dp", "seq")),
            P("dp", "seq", None),
        ),
        out_specs=(
            P("dp", "seq", None),
            P("dp", "seq", None),
            P("dp", None),
            P("dp", "seq"),
            P(("dp", "seq")),
            P("dp", "seq"),
            P(("dp", "seq")),
            P(("dp", "seq")),
            P("dp", "seq"),
            P(("dp", "seq")),
            P("dp", "seq"),
            P(("dp", "seq")),
            P("dp", "seq"),
            P(("dp", "seq")),
        ),
        check_vma=False,
    )
```

```python
import functools

import jax
import jax.numpy as jnp
from jax import lax
from jax.experimental import pallas as pl
from jax.experimental.pallas import tpu as pltpu
from jax.sharding import PartitionSpec as P

HEADS = 16
LOW = jnp.bfloat16
WIDE = jnp.float32
LOG2E = 1.4426950408889634


def normalize(rows):
    centre = rows - jnp.mean(rows, axis=-1, keepdims=True)
    return centre * lax.rsqrt(jnp.mean(centre * centre, axis=-1, keepdims=True) + 1e-06)


def gelu_tanh(value):
    return jax.nn.gelu(value, approximate=True)


def matmul(left, right):
    return jnp.dot(left, right, preferred_element_type=jnp.float32)


def contract_rows(left, right):
    return lax.dot_general(
        left, right, (((0,), (0,)), ((), ())), preferred_element_type=jnp.float32
    )


def contract_cols(left, right):
    return lax.dot_general(
        left, right, (((1,), (1,)), ((), ())), preferred_element_type=jnp.float32
    )


def collect_fore(w_ada, w_qkv, w_proj, w_fc1, w_fc2, b_ada, q_bias, v_bias, b_proj, b_fc1, b_fc2):
    inner = (
        lax.all_gather(w_ada, "seq", axis=1, tiled=True),
        lax.all_gather(w_qkv, "seq", axis=1, tiled=True),
        lax.all_gather(w_proj, "seq", axis=1, tiled=True),
        lax.all_gather(w_fc1, "seq", axis=1, tiled=True),
        lax.all_gather(w_fc2, "seq", axis=1, tiled=True),
        lax.all_gather(b_ada, "seq", axis=0, tiled=True),
        lax.all_gather(q_bias, "seq", axis=0, tiled=True),
        lax.all_gather(v_bias, "seq", axis=0, tiled=True),
        lax.all_gather(b_proj, "seq", axis=0, tiled=True),
        lax.all_gather(b_fc1, "seq", axis=0, tiled=True),
        lax.all_gather(b_fc2, "seq", axis=0, tiled=True),
    )
    return (
        lax.all_gather(inner[0], "dp", axis=0, tiled=True),
        lax.all_gather(inner[1], "dp", axis=0, tiled=True),
        lax.all_gather(inner[2], "dp", axis=0, tiled=True),
        lax.all_gather(inner[3], "dp", axis=0, tiled=True),
        lax.all_gather(inner[4], "dp", axis=0, tiled=True),
        lax.all_gather(inner[5], "dp", axis=0, tiled=True),
        lax.all_gather(inner[6], "dp", axis=0, tiled=True),
        lax.all_gather(inner[7], "dp", axis=0, tiled=True),
        lax.all_gather(inner[8], "dp", axis=0, tiled=True),
        lax.all_gather(inner[9], "dp", axis=0, tiled=True),
        lax.all_gather(inner[10], "dp", axis=0, tiled=True),
    )


def collect_back(w_ada, w_qkv, w_proj, w_fc1, w_fc2):
    inner = (
        lax.all_gather(w_ada, "seq", axis=1, tiled=True),
        lax.all_gather(w_qkv, "seq", axis=1, tiled=True),
        lax.all_gather(w_proj, "seq", axis=1, tiled=True),
        lax.all_gather(w_fc1, "seq", axis=1, tiled=True),
        lax.all_gather(w_fc2, "seq", axis=1, tiled=True),
    )
    return (
        lax.all_gather(inner[0], "dp", axis=0, tiled=True),
        lax.all_gather(inner[1], "dp", axis=0, tiled=True),
        lax.all_gather(inner[2], "dp", axis=0, tiled=True),
        lax.all_gather(inner[3], "dp", axis=0, tiled=True),
        lax.all_gather(inner[4], "dp", axis=0, tiled=True),
    )


def general_body(
    tokens,
    condition,
    w_ada,
    b_ada,
    w_qkv,
    q_bias,
    v_bias,
    w_proj,
    b_proj,
    w_fc1,
    b_fc1,
    w_fc2,
    b_fc2,
    cotangent,
):
    latents_here, tokens_here, model_width = tokens.shape
    head_count = HEADS
    head_size = model_width // head_count
    score_scale = head_size ** (-0.5)
    row_count = latents_here * tokens_here
    gathered = collect_fore(
        w_ada, w_qkv, w_proj, w_fc1, w_fc2, b_ada, q_bias, v_bias, b_proj, b_fc1, b_fc2
    )
    full_ada, full_qkv, full_proj, full_fc1, full_fc2 = (
        gathered[0],
        gathered[1],
        gathered[2],
        gathered[3],
        gathered[4],
    )
    bias_ada = gathered[5].astype(jnp.float32)
    bias_query = gathered[6].astype(jnp.float32)
    bias_value = gathered[7].astype(jnp.float32)
    bias_proj = gathered[8].astype(jnp.float32)
    bias_fc1 = gathered[9].astype(jnp.float32)
    bias_fc2 = gathered[10].astype(jnp.float32)
    inputs = tokens.astype(jnp.float32)
    smooth, silu_pull = jax.vjp(jax.nn.silu, condition)
    smooth_low = smooth.astype(jnp.bfloat16)
    mods = matmul(smooth_low, full_ada) + bias_ada
    pieces = [mods[:, None, index * model_width : (index + 1) * model_width] for index in range(6)]
    shift_one, scale_one, gate_one, shift_two, scale_two, gate_two = pieces
    normed_one, norm_pull_one = jax.vjp(normalize, inputs)
    first_rows = (
        (normed_one * (1.0 + scale_one) + shift_one)
        .astype(jnp.bfloat16)
        .reshape(row_count, model_width)
    )
    bias_row = jnp.concatenate([bias_query, jnp.zeros_like(bias_query), bias_value])
    projected = matmul(first_rows, full_qkv) + bias_row
    query = (
        projected[:, :model_width]
        .astype(jnp.bfloat16)
        .reshape(latents_here, tokens_here, head_count, head_size)
    )
    key_local = (
        projected[:, model_width : 2 * model_width]
        .astype(jnp.bfloat16)
        .reshape(latents_here, tokens_here, model_width)
    )
    value_local = (
        projected[:, 2 * model_width :]
        .astype(jnp.bfloat16)
        .reshape(latents_here, tokens_here, model_width)
    )
    key_all, value_all = (
        lax.all_gather(key_local, "seq", axis=1, tiled=True),
        lax.all_gather(value_local, "seq", axis=1, tiled=True),
    )
    key_count = key_all.shape[1]
    key_heads = key_all.reshape(latents_here, key_count, head_count, head_size)
    value_heads = value_all.reshape(latents_here, key_count, head_count, head_size)
    scores = (
        jnp.einsum("bqhd,bkhd->bhqk", query, key_heads, preferred_element_type=jnp.float32)
        * score_scale
    )
    peak = jnp.max(scores, axis=-1, keepdims=True)
    log_total = jnp.log(jnp.sum(jnp.exp(scores - peak), axis=-1, keepdims=True)) + peak
    softmaxed = jnp.exp(scores - log_total)
    attended = jnp.einsum(
        "bhqk,bkhd->bqhd",
        softmaxed.astype(jnp.bfloat16),
        value_heads,
        preferred_element_type=jnp.float32,
    )
    attended = attended.astype(jnp.bfloat16).reshape(row_count, model_width)
    attention = (matmul(attended, full_proj) + bias_proj).reshape(
        latents_here, tokens_here, model_width
    )
    middle = inputs + gate_one * attention
    normed_two, norm_pull_two = jax.vjp(normalize, middle)
    second_rows = (
        (normed_two * (1.0 + scale_two) + shift_two)
        .astype(jnp.bfloat16)
        .reshape(row_count, model_width)
    )
    hidden = matmul(second_rows, full_fc1) + bias_fc1
    active, gelu_pull = jax.vjp(gelu_tanh, hidden)
    active_low = active.astype(jnp.bfloat16)
    branch = (matmul(active_low, full_fc2) + bias_fc2).reshape(
        latents_here, tokens_here, model_width
    )
    output = (middle + gate_two * branch).astype(jnp.bfloat16)
    regained = collect_back(w_ada, w_qkv, w_proj, w_fc1, w_fc2)
    full_ada, full_qkv, full_proj, full_fc1, full_fc2 = (
        regained[0],
        regained[1],
        regained[2],
        regained[3],
        regained[4],
    )
    grad_out = cotangent.astype(jnp.float32)
    gate_two_grad = jnp.sum(grad_out * branch, axis=1)
    branch_grad = (gate_two * grad_out).astype(jnp.bfloat16).reshape(row_count, model_width)
    fc2_bias_grad = jnp.sum(branch_grad.astype(jnp.float32), axis=0)
    fc2_grad = contract_rows(active_low, branch_grad)
    active_grad = contract_cols(branch_grad, full_fc2)
    hidden_grad = gelu_pull(active_grad)[0].astype(jnp.bfloat16)
    fc1_bias_grad = jnp.sum(hidden_grad.astype(jnp.float32), axis=0)
    fc1_grad = contract_rows(second_rows, hidden_grad)
    second_grad = contract_cols(hidden_grad, full_fc1).reshape(
        latents_here, tokens_here, model_width
    )
    shift_two_grad = jnp.sum(second_grad, axis=1)
    scale_two_grad = jnp.sum(second_grad * normed_two, axis=1)
    middle_grad = grad_out + norm_pull_two(second_grad * (1.0 + scale_two))[0]
    gate_one_grad = jnp.sum(middle_grad * attention, axis=1)
    attention_grad = (gate_one * middle_grad).astype(jnp.bfloat16).reshape(row_count, model_width)
    proj_bias_grad = jnp.sum(attention_grad.astype(jnp.float32), axis=0)
    proj_grad = contract_rows(attended, attention_grad)
    attended_grad = contract_cols(attention_grad, full_proj).astype(jnp.bfloat16)
    attended_grad = attended_grad.reshape(latents_here, tokens_here, head_count, head_size)
    scores = (
        jnp.einsum("bqhd,bkhd->bhqk", query, key_heads, preferred_element_type=jnp.float32)
        * score_scale
    )
    softmaxed = jnp.exp(scores - log_total)
    weight_grad = jnp.einsum(
        "bqhd,bkhd->bhqk", attended_grad, value_heads, preferred_element_type=jnp.float32
    )
    row_delta = jnp.sum(softmaxed * weight_grad, axis=-1, keepdims=True)
    score_grad = (softmaxed * (weight_grad - row_delta)).astype(jnp.bfloat16)
    query_grad = (
        jnp.einsum("bhqk,bkhd->bqhd", score_grad, key_heads, preferred_element_type=jnp.float32)
        * score_scale
    )
    key_grad = (
        jnp.einsum("bhqk,bqhd->bkhd", score_grad, query, preferred_element_type=jnp.float32)
        * score_scale
    )
    value_grad = jnp.einsum(
        "bhqk,bqhd->bkhd",
        softmaxed.astype(jnp.bfloat16),
        attended_grad,
        preferred_element_type=jnp.float32,
    )
    key_mine, value_mine = (
        lax.psum_scatter(
            key_grad.reshape(latents_here, key_count, model_width).astype(jnp.bfloat16),
            "seq",
            scatter_dimension=1,
            tiled=True,
        ).astype(jnp.float32),
        lax.psum_scatter(
            value_grad.reshape(latents_here, key_count, model_width).astype(jnp.bfloat16),
            "seq",
            scatter_dimension=1,
            tiled=True,
        ).astype(jnp.float32),
    )
    query_low = query_grad.astype(jnp.bfloat16).reshape(row_count, model_width)
    value_low = value_mine.astype(jnp.bfloat16).reshape(row_count, model_width)
    joint_grad = jnp.concatenate(
        [query_low, key_mine.astype(jnp.bfloat16).reshape(row_count, model_width), value_low],
        axis=-1,
    )
    query_bias_grad = jnp.sum(query_low.astype(jnp.float32), axis=0)
    value_bias_grad = jnp.sum(value_low.astype(jnp.float32), axis=0)
    qkv_grad = contract_rows(first_rows, joint_grad)
    first_grad = contract_cols(joint_grad, full_qkv).reshape(latents_here, tokens_here, model_width)
    shift_one_grad = jnp.sum(first_grad, axis=1)
    scale_one_grad = jnp.sum(first_grad * normed_one, axis=1)
    input_grad = middle_grad + norm_pull_one(first_grad * (1.0 + scale_one))[0]
    mods_grad = jnp.concatenate(
        [
            shift_one_grad,
            scale_one_grad,
            gate_one_grad,
            shift_two_grad,
            scale_two_grad,
            gate_two_grad,
        ],
        axis=-1,
    )
    mods_low = lax.psum(mods_grad.astype(jnp.bfloat16), "seq")
    leader = (lax.axis_index("seq") == 0).astype(jnp.float32)
    ada_grad = contract_rows(smooth_low, mods_low) * leader
    ada_bias_grad = jnp.sum(mods_low.astype(jnp.float32), axis=0) * leader
    smooth_grad = contract_cols(mods_low, full_ada)
    condition_grad = silu_pull(smooth_grad)[0]
    summed = (
        lax.psum_scatter(
            ada_grad.astype(jnp.bfloat16), "dp", scatter_dimension=0, tiled=True
        ).astype(jnp.float32),
        lax.psum_scatter(
            qkv_grad.astype(jnp.bfloat16), "dp", scatter_dimension=0, tiled=True
        ).astype(jnp.float32),
        lax.psum_scatter(
            proj_grad.astype(jnp.bfloat16), "dp", scatter_dimension=0, tiled=True
        ).astype(jnp.float32),
        lax.psum_scatter(
            fc1_grad.astype(jnp.bfloat16), "dp", scatter_dimension=0, tiled=True
        ).astype(jnp.float32),
        lax.psum_scatter(
            fc2_grad.astype(jnp.bfloat16), "dp", scatter_dimension=0, tiled=True
        ).astype(jnp.float32),
        lax.psum_scatter(
            ada_bias_grad.astype(jnp.bfloat16), "dp", scatter_dimension=0, tiled=True
        ).astype(jnp.float32),
        lax.psum_scatter(
            query_bias_grad.astype(jnp.bfloat16), "dp", scatter_dimension=0, tiled=True
        ).astype(jnp.float32),
        lax.psum_scatter(
            value_bias_grad.astype(jnp.bfloat16), "dp", scatter_dimension=0, tiled=True
        ).astype(jnp.float32),
        lax.psum_scatter(
            proj_bias_grad.astype(jnp.bfloat16), "dp", scatter_dimension=0, tiled=True
        ).astype(jnp.float32),
        lax.psum_scatter(
            fc1_bias_grad.astype(jnp.bfloat16), "dp", scatter_dimension=0, tiled=True
        ).astype(jnp.float32),
        lax.psum_scatter(
            fc2_bias_grad.astype(jnp.bfloat16), "dp", scatter_dimension=0, tiled=True
        ).astype(jnp.float32),
    )
    owned = (
        lax.psum_scatter(
            summed[0].astype(jnp.bfloat16), "seq", scatter_dimension=1, tiled=True
        ).astype(jnp.float32),
        lax.psum_scatter(
            summed[1].astype(jnp.bfloat16), "seq", scatter_dimension=1, tiled=True
        ).astype(jnp.float32),
        lax.psum_scatter(
            summed[2].astype(jnp.bfloat16), "seq", scatter_dimension=1, tiled=True
        ).astype(jnp.float32),
        lax.psum_scatter(
            summed[3].astype(jnp.bfloat16), "seq", scatter_dimension=1, tiled=True
        ).astype(jnp.float32),
        lax.psum_scatter(
            summed[4].astype(jnp.bfloat16), "seq", scatter_dimension=1, tiled=True
        ).astype(jnp.float32),
        lax.psum_scatter(
            summed[5].astype(jnp.bfloat16), "seq", scatter_dimension=0, tiled=True
        ).astype(jnp.float32),
        lax.psum_scatter(
            summed[6].astype(jnp.bfloat16), "seq", scatter_dimension=0, tiled=True
        ).astype(jnp.float32),
        lax.psum_scatter(
            summed[7].astype(jnp.bfloat16), "seq", scatter_dimension=0, tiled=True
        ).astype(jnp.float32),
        lax.psum_scatter(
            summed[8].astype(jnp.bfloat16), "seq", scatter_dimension=0, tiled=True
        ).astype(jnp.float32),
        lax.psum_scatter(
            summed[9].astype(jnp.bfloat16), "seq", scatter_dimension=0, tiled=True
        ).astype(jnp.float32),
        lax.psum_scatter(
            summed[10].astype(jnp.bfloat16), "seq", scatter_dimension=0, tiled=True
        ).astype(jnp.float32),
    )
    return (
        output,
        input_grad,
        condition_grad,
        owned[0],
        owned[5],
        owned[1],
        owned[6],
        owned[7],
        owned[2],
        owned[8],
        owned[3],
        owned[9],
        owned[4],
        owned[10],
    )


NT = (((1,), (1,)), ((), ()))
NN = (((1,), (0,)), ((), ()))


def product(left, right, dims):
    return lax.dot_general(left, right, dims, preferred_element_type=WIDE)


def flat(ref):
    value = ref[...]
    return value.reshape(value.shape[0] * value.shape[2], value.shape[3])


def attention_kernel(q_ref, k_ref, v_ref, o_ref, e_ref, r_ref, *, size, chunk):
    q, k, v = flat(q_ref), flat(k_ref), flat(v_ref)
    count = q.shape[0]
    scaled = q.astype(WIDE) * (LOG2E * size**-0.5)
    high = scaled.astype(LOW)
    rest = (scaled - high.astype(WIDE)).astype(LOW)
    v_t = v.astype(WIDE).T.astype(LOW)
    ones = jnp.ones((16, count), LOW)
    outs, inverses = [], []
    for head in range(q.shape[1] // size):
        cols = slice(head * size, (head + 1) * size)
        keys = jnp.concatenate([k[:, cols], k[:, cols]], 1)
        queries = jnp.concatenate([high[:, cols], rest[:, cols]], 1)
        values = jnp.concatenate([v_t[cols], ones], 0)
        out_parts, inverse_parts = [], []
        for at in range(0, count, chunk):
            scores = product(keys, queries[at : at + chunk], NT)
            peak = jnp.max(scores, axis=0, keepdims=True)
            weights = jnp.exp2(scores - peak).astype(LOW)
            e_ref[0, 0, head, :, at : at + chunk] = weights
            summed = product(values, weights, NN)
            inverse = 1.0 / summed[size : size + 1]
            out_parts.append(summed[:size] * inverse)
            inverse_parts.append(inverse)
        outs.append(jnp.concatenate(out_parts, 1))
        inverses.append(jnp.concatenate(inverse_parts, 1))
    o_ref[...] = jnp.concatenate(outs, 0).T.astype(LOW).reshape(o_ref.shape)
    r_ref[0, 0] = jnp.concatenate(inverses, 0)


def attention_back_kernel(
    q_ref, k_ref, v_ref, o_ref, do_ref, e_ref, r_ref, dq_ref, dk_ref, dv_ref, *, size
):
    q, k, v = flat(q_ref), flat(k_ref), flat(v_ref)
    do, o = flat(do_ref).astype(WIDE), flat(o_ref).astype(WIDE)
    scale = size**-0.5
    inverse = r_ref[0, 0]
    prod_t = (do * o).T
    do_t = do.T
    k_t = (k.astype(WIDE) * scale).T.astype(LOW)
    q_scaled = (q.astype(WIDE) * scale).astype(LOW)
    dqs, dks, dvs = [], [], []
    for head in range(q.shape[1] // size):
        cols = slice(head * size, (head + 1) * size)
        inv = inverse[head : head + 1]
        grad_t = do_t[cols] * inv
        delta = jnp.sum(prod_t[cols], axis=0, keepdims=True) * inv
        weights = e_ref[0, 0, head]
        da = product(v[:, cols], grad_t.astype(LOW), NN)
        ds = weights * (da - delta).astype(LOW)
        dqs.append(product(k_t[cols], ds, NN))
        dks.append(product(ds, q_scaled[:, cols], NN))
        dvs.append(product(weights, grad_t.T.astype(LOW), NN))
    dq_ref[...] = jnp.concatenate(dqs, 0).T.astype(LOW).reshape(dq_ref.shape)
    dk_ref[...] = jnp.concatenate(dks, 1).astype(LOW).reshape(dk_ref.shape)
    dv_ref[...] = jnp.concatenate(dvs, 1).astype(LOW).reshape(dv_ref.shape)


PARAMS = pltpu.CompilerParams(vmem_limit_bytes=56 << 20)


def attention_blocks(half, tokens, width):
    def columns(base):
        return pl.BlockSpec((half, 1, tokens, width), lambda latent, pair: (0, latent, 0, base + pair))

    return columns


def attention_fore(qkv):
    half, latents, tokens, triple = qkv.shape
    model = triple // 3
    size = model // HEADS
    per = 128 // size
    pairs = HEADS // per
    count = half * tokens
    columns = attention_blocks(half, tokens, 128)
    flops = 4 * latents * HEADS * count * count * 128
    return pl.pallas_call(
        functools.partial(attention_kernel, size=size, chunk=count),
        grid=(latents, pairs),
        in_specs=[columns(0), columns(pairs), columns(2 * pairs)],
        out_specs=[
            columns(0),
            pl.BlockSpec((1, 1, per, count, count), lambda latent, pair: (latent, pair, 0, 0, 0)),
            pl.BlockSpec((1, 1, per, count), lambda latent, pair: (latent, pair, 0, 0)),
        ],
        out_shape=[
            jax.ShapeDtypeStruct((half, latents, tokens, model), LOW),
            jax.ShapeDtypeStruct((latents, pairs, per, count, count), LOW),
            jax.ShapeDtypeStruct((latents, pairs, per, count), WIDE),
        ],
        compiler_params=PARAMS,
        cost_estimate=pl.CostEstimate(
            flops=flops, bytes_accessed=90 << 20, transcendentals=latents * HEADS * count * count
        ),
        name="attention_fore",
    )(qkv, qkv, qkv)


def attention_back(qkv, attended, attended_grad, weights, inverse):
    half, latents, tokens, triple = qkv.shape
    model = triple // 3
    size = model // HEADS
    per = 128 // size
    pairs = HEADS // per
    count = half * tokens
    columns = attention_blocks(half, tokens, 128)
    flops = 8 * latents * HEADS * count * count * 128
    grads = jax.ShapeDtypeStruct((half, latents, tokens, model), LOW)
    return pl.pallas_call(
        functools.partial(attention_back_kernel, size=size),
        grid=(latents, pairs),
        in_specs=[
            columns(0),
            columns(pairs),
            columns(2 * pairs),
            columns(0),
            columns(0),
            pl.BlockSpec((1, 1, per, count, count), lambda latent, pair: (latent, pair, 0, 0, 0)),
            pl.BlockSpec((1, 1, per, count), lambda latent, pair: (latent, pair, 0, 0)),
        ],
        out_specs=[columns(0)] * 3,
        out_shape=[grads] * 3,
        compiler_params=PARAMS,
        cost_estimate=pl.CostEstimate(flops=flops, bytes_accessed=100 << 20, transcendentals=0),
        name="attention_back",
    )(qkv, qkv, qkv, attended, attended_grad, weights, inverse)


SIX = 6


def norm_parts(rows):
    centre = rows - jnp.mean(rows, axis=1, keepdims=True)
    inverse = lax.rsqrt(jnp.mean(centre * centre, axis=1, keepdims=True) + 1e-06)
    return centre * inverse, inverse


def norm_back(grad, normed, inverse):
    mean = jnp.mean(grad, axis=1, keepdims=True)
    along = jnp.mean(grad * normed, axis=1, keepdims=True)
    return (grad - mean - normed * along) * inverse


def down_sum(value):
    return jnp.sum(value, axis=0, keepdims=True)


def accumulate(ref, value, start):
    @pl.when(start)
    def _():
        ref[...] = value.reshape(ref.shape)

    @pl.when(jnp.logical_not(start))
    def _():
        ref[...] += value.reshape(ref.shape)


def first_of_latent():
    return (pl.program_id(1) == 0) & (pl.program_id(2) == 0)


def first_of_all():
    return (pl.program_id(0) == 0) & first_of_latent()


def project_kernel(x_ref, mods_ref, w_ref, bias_ref, first_ref, qkv_ref):
    mods = mods_ref[0]
    normed, _ = norm_parts(x_ref[0, 0].astype(WIDE))
    first = (normed * (1.0 + mods[1:2]) + mods[0:1]).astype(LOW)
    first_ref[0, 0] = first
    model = first.shape[1]
    for at in range(0, 3 * model, model):
        cols = slice(at, at + model)
        qkv_ref[0, 0, :, cols] = (product(first, w_ref[:, cols], NN) + bias_ref[:, cols]).astype(LOW)


def forward_kernel(
    x_ref, o_ref, dy_ref, mods_ref, w_proj_ref, b_proj_ref, w1_ref, b1_ref, w2_ref, b2_ref,
    out_ref, second_ref, active_ref, slope_ref, attention_ref, middle_ref, dm_ref, gate_ref,
):
    mods = mods_ref[0]
    attention = product(o_ref[0, 0], w_proj_ref[...], NN) + b_proj_ref[...]
    attention_ref[0, 0] = attention.astype(LOW)
    middle = x_ref[0, 0].astype(WIDE) + mods[2:3] * attention
    middle_ref[0, 0] = middle
    normed, _ = norm_parts(middle)
    second = (normed * (1.0 + mods[4:5]) + mods[3:4]).astype(LOW)
    second_ref[0, 0] = second
    branch = b2_ref[...]
    width = second.shape[1]
    for at in range(0, w1_ref.shape[1], width):
        cols = slice(at, at + width)
        hidden = product(second, w1_ref[:, cols], NN) + b1_ref[:, cols]
        square = hidden * hidden
        bend = jnp.tanh(hidden * (0.7978845608028654 + 0.035677408136300125 * square))
        half = 0.5 + 0.5 * bend
        active = (hidden * half).astype(LOW)
        steep = 0.7978845608028654 + 0.10703222440890037 * square
        slope = half + (0.5 * hidden) * (1.0 - bend * bend) * steep
        active_ref[0, 0, :, cols] = active
        slope_ref[0, 0, :, cols] = slope.astype(LOW)
        branch = branch + product(active, w2_ref[cols, :], NN)
    out_ref[0, 0] = (middle + mods[5:6] * branch).astype(LOW)
    dy = dy_ref[0, 0].astype(WIDE)
    dm_ref[0, 0] = (mods[5:6] * dy).astype(LOW)
    accumulate(gate_ref, down_sum(dy * branch), first_of_latent())


def backward_kernel(
    dy_ref, dm_ref, slope_ref, middle_ref, attention_ref, mods_ref, w_proj_ref, w1_ref, w2_ref,
    dh_ref, dmiddle_ref, dattention_ref, do_ref, sums_ref, b1_ref, b2_ref, b_proj_ref,
):
    mods = mods_ref[0]
    dm = dm_ref[0, 0]
    width = dm.shape[1]
    start = first_of_all()
    dsecond = None
    for at in range(0, w1_ref.shape[1], width):
        cols = slice(at, at + width)
        dh = (product(dm, w2_ref[cols, :], NT) * slope_ref[0, 0, :, cols].astype(WIDE)).astype(LOW)
        dh_ref[0, 0, :, cols] = dh
        accumulate(b1_ref.at[:, cols], down_sum(dh.astype(WIDE)), start)
        part = product(dh, w1_ref[:, cols], NT)
        dsecond = part if dsecond is None else dsecond + part
    normed, inverse = norm_parts(middle_ref[0, 0])
    dmiddle = dy_ref[0, 0].astype(WIDE) + norm_back(dsecond * (1.0 + mods[4:5]), normed, inverse)
    dmiddle_ref[0, 0] = dmiddle
    dattention = (mods[2:3] * dmiddle).astype(LOW)
    dattention_ref[0, 0] = dattention
    do_ref[0, 0] = product(dattention, w_proj_ref[...], NT).astype(LOW)
    sums = jnp.concatenate(
        [
            down_sum(dmiddle * attention_ref[0, 0].astype(WIDE)),
            down_sum(dsecond),
            down_sum(dsecond * normed),
        ],
        axis=0,
    )
    accumulate(sums_ref, sums, first_of_latent())
    accumulate(b2_ref, down_sum(dm.astype(WIDE)), start)
    accumulate(b_proj_ref, down_sum(dattention.astype(WIDE)), start)


def project_back_kernel(
    dq_ref, dk_ref, dv_ref, x_ref, dmiddle_ref, mods_ref, w_ref, dx_ref, sums_ref, bq_ref, bv_ref
):
    mods = mods_ref[0]
    model = x_ref.shape[3]
    grads = [dq_ref[0, 0], dk_ref[0, 0], dv_ref[0, 0]]
    dfirst = sum(
        product(grad, w_ref[:, i * model : (i + 1) * model], NT) for i, grad in enumerate(grads)
    )
    normed, inverse = norm_parts(x_ref[0, 0].astype(WIDE))
    dx_ref[0, 0] = dmiddle_ref[0, 0] + norm_back(dfirst * (1.0 + mods[1:2]), normed, inverse)
    sums = jnp.concatenate([down_sum(dfirst), down_sum(dfirst * normed)], axis=0)
    accumulate(sums_ref, sums, first_of_latent())
    start = first_of_all()
    accumulate(bq_ref, down_sum(grads[0].astype(WIDE)), start)
    accumulate(bv_ref, down_sum(grads[2].astype(WIDE)), start)


def row_call(kernel, like, operands, results, flops, name, span):
    half, latents, tokens, _ = like.shape
    span = min(span, tokens)

    def spec(shape, kind):
        if kind == "rows":
            return pl.BlockSpec((1, 1, span, shape[3]), lambda l, h, i: (h, l, i, 0))
        if kind == "latent":
            return pl.BlockSpec((1,) + shape[1:], lambda l, h, i: (l,) + (0,) * (len(shape) - 1))
        width, index = kind
        return pl.BlockSpec(
            (shape[0], width), lambda l, h, i: (0, index), pipeline_mode=pl.Buffered(1)
        )

    def out_spec(shape, kind):
        if kind == "all":
            return pl.BlockSpec(shape, lambda l, h, i: (0, 0))
        return spec(shape, kind)

    return pl.pallas_call(
        kernel,
        grid=(latents, half, tokens // span),
        in_specs=[spec(a.shape, kind) for a, kind in operands],
        out_specs=[out_spec(shape, kind) for shape, _, kind in results],
        out_shape=[jax.ShapeDtypeStruct(shape, dtype) for shape, dtype, _ in results],
        compiler_params=PARAMS,
        cost_estimate=pl.CostEstimate(flops=flops, bytes_accessed=64 << 20, transcendentals=0),
        name=name,
    )(*(a for a, _ in operands))


class Wires:
    def __init__(self, dp):
        self.depth = dp // 4
        index = lax.axis_index("dp")
        self.z, self.y, self.core = index // 4, (index // 2) % 2, index % 2
        self.x = lax.axis_index("seq")
        self.places = [(z, y, c) for z in range(self.depth) for y in range(2) for c in range(2)]

    def across(self, value):
        return lax.ppermute(value, "seq", [(0, 1), (1, 0)])

    def dp_step(self, value, move):
        pairs = []
        for z, y, c in self.places:
            to_z, to_y, to_c = move(z, y, c)
            pairs.append(((z * 2 + y) * 2 + c, (to_z * 2 + to_y) * 2 + to_c))
        return lax.ppermute(value, "dp", pairs)

    def distances(self):
        steps, distance = [], self.depth // 2
        while distance:
            steps.append(distance)
            distance //= 2
        return steps

    def bit(self, distance):
        return (self.z // distance) % 2

    def mirror(self, value, distance):
        return self.dp_step(value, lambda z, y, c: (z ^ distance, y, c))

    def beside(self, value):
        return self.dp_step(value, lambda z, y, c: (z, 1 - y, c))

    def twin(self, value):
        return self.dp_step(value, lambda z, y, c: (z, y, 1 - c))


def pick(value, index, axis):
    return lax.dynamic_index_in_dim(value, index, axis, keepdims=False)


def order_two(mine, other, index, axis, fresh=False):
    if fresh:
        mine, other = mine[:, None], other[:, None]
        both = order_two(mine, other, index, 1)
        return both.reshape((-1,) + both.shape[2:])
    return jnp.where(
        index == 0,
        jnp.concatenate([mine, other], axis),
        jnp.concatenate([other, mine], axis),
    )


def gather_line(wires, value):
    held = value[None]
    for distance in wires.distances():
        held = order_two(held, wires.mirror(held, distance), wires.bit(distance), 0, True)
    return held


def gather_small(wires, value):
    held = gather_line(wires, value)
    held = order_two(held, wires.beside(held), wires.y, 0, True)
    held = order_two(held, wires.twin(held), wires.core, 0, True)
    return held


def sum_small(wires, value):
    held = value.reshape((wires.depth, 2, 2) + value.shape[1:])
    held = pick(held, wires.core, 2) + wires.twin(pick(held, 1 - wires.core, 2))
    return sum_planes(wires, held)


def sum_planes(wires, held):
    held = pick(held, wires.y, 1) + wires.beside(pick(held, 1 - wires.y, 1))
    distances = wires.distances()
    held = held.reshape((2,) * len(distances) + held.shape[1:])
    for place, distance in reversed(list(enumerate(distances))):
        bit = wires.bit(distance)
        held = pick(held, bit, place) + wires.mirror(pick(held, 1 - bit, place), distance)
    return held


def gather_weight(shard):
    return lax.all_gather(shard, "dp", axis=0, tiled=True)


def scatter_grad(wires, grad):
    return split_columns(wires, lax.psum_scatter(grad, "dp", scatter_dimension=0, tiled=True))


def split_columns(wires, held):
    halves = held.reshape(held.shape[0], 2, held.shape[1] // 2)
    theirs = wires.across(pick(halves, 1 - wires.x, 1))
    return pick(halves, wires.x, 1).astype(WIDE) + theirs.astype(WIDE)


def fast_body(
    dp,
    tokens,
    condition,
    w_ada,
    b_ada,
    w_qkv,
    q_bias,
    v_bias,
    w_proj,
    b_proj,
    w_fc1,
    b_fc1,
    w_fc2,
    b_fc2,
    cotangent,
):
    wires = Wires(dp)
    group, tokens_here, model = tokens.shape
    mine = group // 2
    rows = group * tokens_here
    x, z_y_c = wires.x, lax.axis_index("dp")

    def swap(value):
        ours = lax.dynamic_slice_in_dim(value, x * mine, mine, 0)
        theirs = lax.dynamic_slice_in_dim(value, (1 - x) * mine, mine, 0)
        return ours, wires.across(theirs)

    def swap_back(value, theirs):
        return order_two(value[0], theirs.astype(value.dtype), x, 0)

    packed = jnp.concatenate([w_qkv, w_proj, w_fc1], axis=1)
    theirs = wires.across(packed)
    cuts = [w_qkv.shape[1], w_qkv.shape[1] + w_proj.shape[1]]
    own_qkv, own_proj, own_fc1 = (
        order_two(a, b, x, 1) for a, b in zip(jnp.split(packed, cuts, 1), jnp.split(theirs, cuts, 1))
    )
    own_fc2 = order_two(w_fc2, wires.across(w_fc2), x, 1)
    full_qkv = gather_weight(own_qkv)
    full_both = gather_weight(jnp.concatenate([own_fc1, own_proj], axis=1))
    lines_fc2 = gather_line(wires, own_fc2)
    tokens_two = jnp.stack(swap(tokens))

    vectors = (q_bias, v_bias, b_proj, b_fc1, b_fc2, b_ada)
    sizes = [v.shape[0] for v in vectors]
    offsets = [sum(sizes[:i]) for i in range(len(sizes))]
    biases = jnp.concatenate(vectors)[None]
    biases = order_two(biases, wires.across(biases), x, 0)
    smooth, silu_pull = jax.vjp(jax.nn.silu, condition)
    smooth_low = smooth.astype(LOW)
    vector = jnp.concatenate([smooth_low.reshape(-1), biases.reshape(-1)])
    vector = gather_small(wires, vector)
    joined = vector[:, group * model :].reshape(2 * dp, -1)
    bias_query, bias_value, bias_proj, bias_fc1, bias_fc2, bias_ada = (
        joined[:, o : o + n].reshape(-1).astype(WIDE) for o, n in zip(offsets, sizes)
    )

    smooth_all = vector[:, : group * model].reshape(dp * group, model)
    ada_rows = w_ada.shape[0]
    smooth_mine = lax.dynamic_slice_in_dim(smooth_all, z_y_c * ada_rows, ada_rows, 1)
    partial = matmul(smooth_mine, w_ada)
    half_mods = sum_small(wires, partial.reshape(dp, group, -1))
    ours, theirs = swap(half_mods)
    mods = order_two(ours, theirs, x, 1) + bias_ada
    mods = mods.reshape(mine, SIX, model)
    hidden_width = dp * w_fc2.shape[0]
    rows4 = lambda width: (2, mine, tokens_here, width)
    bias_row = jnp.concatenate([bias_query, jnp.zeros_like(bias_query), bias_value])[None]
    first, qkv = row_call(
        project_kernel,
        tokens_two,
        [
            (tokens_two, "rows"),
            (mods, "latent"),
            (full_qkv, (3 * model, 0)),
            (bias_row, (3 * model, 0)),
        ],
        [(rows4(model), LOW, "rows"), (rows4(3 * model), LOW, "rows")],
        6 * rows * model * model,
        "project",
        512,
    )
    cotangent, lines_fc2, w_ada, qkv = lax.optimization_barrier((cotangent, lines_fc2, w_ada, qkv))
    ada_across, lines_beside = wires.across(w_ada), wires.beside(lines_fc2)
    ours, theirs = swap(cotangent)
    attended, weights, inverse = attention_fore(qkv)
    ada_across, lines_beside, theirs, attended = lax.optimization_barrier(
        (ada_across, lines_beside, theirs, attended)
    )
    both_ada = order_two(w_ada, ada_across, x, 1)
    cotangent_two = jnp.stack([ours, theirs])
    planes_fc2 = order_two(lines_fc2, lines_beside, wires.y, 0, True)
    full_fc2 = order_two(planes_fc2, wires.twin(planes_fc2), wires.core, 0, True)
    full_fc2 = full_fc2.reshape(-1, model)
    (output, second, active, slope, attention, middle, branch_grad, gate_two_grad) = row_call(
        forward_kernel,
        tokens_two,
        [
            (tokens_two, "rows"),
            (attended, "rows"),
            (cotangent_two, "rows"),
            (mods, "latent"),
            (full_both, (model, hidden_width // model)),
            (bias_proj[None], (model, 0)),
            (full_both, (hidden_width, 0)),
            (bias_fc1[None], (hidden_width, 0)),
            (full_fc2, (model, 0)),
            (bias_fc2[None], (model, 0)),
        ],
        [
            (rows4(model), LOW, "rows"),
            (rows4(model), LOW, "rows"),
            (rows4(hidden_width), LOW, "rows"),
            (rows4(hidden_width), LOW, "rows"),
            (rows4(model), LOW, "rows"),
            (rows4(model), WIDE, "rows"),
            (rows4(model), LOW, "rows"),
            ((mine, 1, model), WIDE, "latent"),
        ],
        2 * rows * model * (model + 2 * hidden_width),
        "forward",
        256,
    )

    def flat_rows(value):
        return value.reshape(rows, value.shape[-1])

    output_across = wires.across(output[1])
    fc2_grad = contract_rows(flat_rows(active), flat_rows(branch_grad)).astype(LOW)
    branch_grad, fc2_grad = lax.optimization_barrier((branch_grad, fc2_grad))
    fc2_rows = lax.psum_scatter(fc2_grad, "dp", scatter_dimension=0, tiled=True)
    (
        hidden_grad,
        middle_grad,
        attention_grad,
        attended_grad,
        middle_sums,
        fc1_bias_grad,
        fc2_bias_grad,
        proj_bias_grad,
    ) = row_call(
        backward_kernel,
        tokens_two,
        [
            (cotangent_two, "rows"),
            (branch_grad, "rows"),
            (slope, "rows"),
            (middle, "rows"),
            (attention, "rows"),
            (mods, "latent"),
            (full_both, (model, hidden_width // model)),
            (full_both, (hidden_width, 0)),
            (full_fc2, (model, 0)),
        ],
        [
            (rows4(hidden_width), LOW, "rows"),
            (rows4(model), WIDE, "rows"),
            (rows4(model), LOW, "rows"),
            (rows4(model), LOW, "rows"),
            ((mine, 3, model), WIDE, "latent"),
            ((1, hidden_width), WIDE, "all"),
            ((1, model), WIDE, "all"),
            ((1, model), WIDE, "all"),
        ],
        2 * rows * model * (model + 2 * hidden_width),
        "backward",
        256,
    )
    fc1_grad = contract_rows(flat_rows(second), flat_rows(hidden_grad)).astype(LOW)
    attention_grad, fc1_grad = lax.optimization_barrier((attention_grad, fc1_grad))
    fc1_rows = lax.psum_scatter(fc1_grad, "dp", scatter_dimension=0, tiled=True)
    proj_grad = contract_rows(flat_rows(attended), flat_rows(attention_grad)).astype(LOW)
    attended_grad, proj_grad, fc2_rows, output_across = lax.optimization_barrier(
        (attended_grad, proj_grad, fc2_rows, output_across)
    )
    output = swap_back(output, output_across)
    fc2_grad = split_columns(wires, fc2_rows)
    dq, dk, dv = attention_back(qkv, attended, attended_grad, weights, inverse)
    joint = jnp.concatenate([flat_rows(d) for d in (dq, dk, dv)], axis=-1)
    qkv_grad = contract_rows(flat_rows(first), joint).astype(LOW)
    qkv_grad = qkv_grad.reshape((wires.depth, 2, 2, -1) + qkv_grad.shape[1:])
    kept, sent = pick(qkv_grad, wires.core, 2), pick(qkv_grad, 1 - wires.core, 2)
    kept = kept + wires.twin(sent)
    dk, kept, fc1_rows = lax.optimization_barrier((dk, kept, fc1_rows))
    proj_grad, fc1_rows = lax.optimization_barrier((proj_grad, fc1_rows))
    proj_grad = scatter_grad(wires, proj_grad)
    fc1_grad = split_columns(wires, fc1_rows)
    qkv_grad = split_columns(wires, sum_planes(wires, kept))
    input_grad, first_sums, query_bias_grad, value_bias_grad = row_call(
        project_back_kernel,
        tokens_two,
        [
            (dq, "rows"),
            (dk, "rows"),
            (dv, "rows"),
            (tokens_two, "rows"),
            (middle_grad, "rows"),
            (mods, "latent"),
            (full_qkv, (3 * model, 0)),
        ],
        [
            (rows4(model), WIDE, "rows"),
            ((mine, 2, model), WIDE, "latent"),
            ((1, model), WIDE, "all"),
            ((1, model), WIDE, "all"),
        ],
        6 * rows * model * model,
        "project_back",
        512,
    )

    mods_grad = jnp.concatenate([first_sums, middle_sums, gate_two_grad], axis=1).astype(LOW)
    mods_grad = mods_grad.reshape(mine, SIX * model)
    sums = (query_bias_grad, value_bias_grad, proj_bias_grad, fc1_bias_grad, fc2_bias_grad)
    bias_sums = jnp.concatenate([v.reshape(2 * dp, -1) for v in sums], axis=1).reshape(dp, 2, -1)
    bias_sums = pick(bias_sums, x, 1) + wires.across(pick(bias_sums, 1 - x, 1))
    group_grad = order_two(mods_grad, wires.across(mods_grad), x, 0)
    input_grad, group_grad, bias_sums = lax.optimization_barrier((input_grad, group_grad, bias_sums))
    input_grad = swap_back(input_grad, wires.across(input_grad[1].astype(LOW)))
    owned = sum_small(wires, bias_sums)
    all_grad = gather_small(wires, group_grad).reshape(dp * group, -1)
    half_grad = lax.dynamic_slice_in_dim(all_grad, x * 3 * model, 3 * model, 1)
    ada_grad = contract_rows(smooth_mine, half_grad)
    ada_bias_grad = lax.dynamic_slice_in_dim(
        jnp.sum(all_grad.astype(WIDE), axis=0), (z_y_c * 2 + x) * b_ada.shape[0], b_ada.shape[0], 0
    )
    smooth_part = contract_cols(all_grad, both_ada)
    spread = lax.all_to_all(
        smooth_part.reshape(dp, group, ada_rows), "dp", 0, 0, tiled=False
    )
    smooth_grad = jnp.swapaxes(spread, 0, 1).reshape(group, model)
    condition_grad = silu_pull(smooth_grad)[0]

    bias_grads = [owned[o : o + n] for o, n in zip(offsets, sizes[:5])]
    return (
        output,
        input_grad,
        condition_grad,
        ada_grad,
        ada_bias_grad,
        qkv_grad,
        bias_grads[0],
        bias_grads[1],
        proj_grad,
        bias_grads[2],
        fc1_grad,
        bias_grads[3],
        fc2_grad,
        bias_grads[4],
    )


def solution(mesh):
    sizes = dict(mesh.shape)

    def body(tokens, *others):
        split = sizes["seq"] == 2 and sizes["dp"] % 4 == 0 and tokens.shape[0] % 2 == 0
        if split:
            return fast_body(sizes["dp"], tokens, *others)
        return general_body(tokens, *others)

    return jax.shard_map(
        body,
        mesh=mesh,
        in_specs=(
            P("dp", "seq", None),
            P("dp", None),
            P("dp", "seq"),
            P(("dp", "seq")),
            P("dp", "seq"),
            P(("dp", "seq")),
            P(("dp", "seq")),
            P("dp", "seq"),
            P(("dp", "seq")),
            P("dp", "seq"),
            P(("dp", "seq")),
            P("dp", "seq"),
            P(("dp", "seq")),
            P("dp", "seq", None),
        ),
        out_specs=(
            P("dp", "seq", None),
            P("dp", "seq", None),
            P("dp", None),
            P("dp", "seq"),
            P(("dp", "seq")),
            P("dp", "seq"),
            P(("dp", "seq")),
            P(("dp", "seq")),
            P("dp", "seq"),
            P(("dp", "seq")),
            P("dp", "seq"),
            P(("dp", "seq")),
            P("dp", "seq"),
            P(("dp", "seq")),
        ),
        check_vma=False,
    )
```

```python
import functools

import jax
import jax.numpy as jnp
from jax import lax
from jax.experimental import pallas as pl
from jax.experimental.pallas import tpu as pltpu
from jax.sharding import PartitionSpec as P

HEADS = 16
LOW = jnp.bfloat16
WIDE = jnp.float32
LOG2E = 1.4426950408889634


def normalize(rows):
    centre = rows - jnp.mean(rows, axis=-1, keepdims=True)
    return centre * lax.rsqrt(jnp.mean(centre * centre, axis=-1, keepdims=True) + 1e-06)


def gelu_tanh(value):
    return jax.nn.gelu(value, approximate=True)


def matmul(left, right):
    return jnp.dot(left, right, preferred_element_type=jnp.float32)


def contract_rows(left, right):
    return lax.dot_general(
        left, right, (((0,), (0,)), ((), ())), preferred_element_type=jnp.float32
    )


def contract_cols(left, right):
    return lax.dot_general(
        left, right, (((1,), (1,)), ((), ())), preferred_element_type=jnp.float32
    )


def collect_fore(w_ada, w_qkv, w_proj, w_fc1, w_fc2, b_ada, q_bias, v_bias, b_proj, b_fc1, b_fc2):
    inner = (
        lax.all_gather(w_ada, "seq", axis=1, tiled=True),
        lax.all_gather(w_qkv, "seq", axis=1, tiled=True),
        lax.all_gather(w_proj, "seq", axis=1, tiled=True),
        lax.all_gather(w_fc1, "seq", axis=1, tiled=True),
        lax.all_gather(w_fc2, "seq", axis=1, tiled=True),
        lax.all_gather(b_ada, "seq", axis=0, tiled=True),
        lax.all_gather(q_bias, "seq", axis=0, tiled=True),
        lax.all_gather(v_bias, "seq", axis=0, tiled=True),
        lax.all_gather(b_proj, "seq", axis=0, tiled=True),
        lax.all_gather(b_fc1, "seq", axis=0, tiled=True),
        lax.all_gather(b_fc2, "seq", axis=0, tiled=True),
    )
    return (
        lax.all_gather(inner[0], "dp", axis=0, tiled=True),
        lax.all_gather(inner[1], "dp", axis=0, tiled=True),
        lax.all_gather(inner[2], "dp", axis=0, tiled=True),
        lax.all_gather(inner[3], "dp", axis=0, tiled=True),
        lax.all_gather(inner[4], "dp", axis=0, tiled=True),
        lax.all_gather(inner[5], "dp", axis=0, tiled=True),
        lax.all_gather(inner[6], "dp", axis=0, tiled=True),
        lax.all_gather(inner[7], "dp", axis=0, tiled=True),
        lax.all_gather(inner[8], "dp", axis=0, tiled=True),
        lax.all_gather(inner[9], "dp", axis=0, tiled=True),
        lax.all_gather(inner[10], "dp", axis=0, tiled=True),
    )


def collect_back(w_ada, w_qkv, w_proj, w_fc1, w_fc2):
    inner = (
        lax.all_gather(w_ada, "seq", axis=1, tiled=True),
        lax.all_gather(w_qkv, "seq", axis=1, tiled=True),
        lax.all_gather(w_proj, "seq", axis=1, tiled=True),
        lax.all_gather(w_fc1, "seq", axis=1, tiled=True),
        lax.all_gather(w_fc2, "seq", axis=1, tiled=True),
    )
    return (
        lax.all_gather(inner[0], "dp", axis=0, tiled=True),
        lax.all_gather(inner[1], "dp", axis=0, tiled=True),
        lax.all_gather(inner[2], "dp", axis=0, tiled=True),
        lax.all_gather(inner[3], "dp", axis=0, tiled=True),
        lax.all_gather(inner[4], "dp", axis=0, tiled=True),
    )


def general_body(
    tokens,
    condition,
    w_ada,
    b_ada,
    w_qkv,
    q_bias,
    v_bias,
    w_proj,
    b_proj,
    w_fc1,
    b_fc1,
    w_fc2,
    b_fc2,
    cotangent,
):
    latents_here, tokens_here, model_width = tokens.shape
    head_count = HEADS
    head_size = model_width // head_count
    score_scale = head_size ** (-0.5)
    row_count = latents_here * tokens_here
    gathered = collect_fore(
        w_ada, w_qkv, w_proj, w_fc1, w_fc2, b_ada, q_bias, v_bias, b_proj, b_fc1, b_fc2
    )
    full_ada, full_qkv, full_proj, full_fc1, full_fc2 = (
        gathered[0],
        gathered[1],
        gathered[2],
        gathered[3],
        gathered[4],
    )
    bias_ada = gathered[5].astype(jnp.float32)
    bias_query = gathered[6].astype(jnp.float32)
    bias_value = gathered[7].astype(jnp.float32)
    bias_proj = gathered[8].astype(jnp.float32)
    bias_fc1 = gathered[9].astype(jnp.float32)
    bias_fc2 = gathered[10].astype(jnp.float32)
    inputs = tokens.astype(jnp.float32)
    smooth, silu_pull = jax.vjp(jax.nn.silu, condition)
    smooth_low = smooth.astype(jnp.bfloat16)
    mods = matmul(smooth_low, full_ada) + bias_ada
    pieces = [mods[:, None, index * model_width : (index + 1) * model_width] for index in range(6)]
    shift_one, scale_one, gate_one, shift_two, scale_two, gate_two = pieces
    normed_one, norm_pull_one = jax.vjp(normalize, inputs)
    first_rows = (
        (normed_one * (1.0 + scale_one) + shift_one)
        .astype(jnp.bfloat16)
        .reshape(row_count, model_width)
    )
    bias_row = jnp.concatenate([bias_query, jnp.zeros_like(bias_query), bias_value])
    projected = matmul(first_rows, full_qkv) + bias_row
    query = (
        projected[:, :model_width]
        .astype(jnp.bfloat16)
        .reshape(latents_here, tokens_here, head_count, head_size)
    )
    key_local = (
        projected[:, model_width : 2 * model_width]
        .astype(jnp.bfloat16)
        .reshape(latents_here, tokens_here, model_width)
    )
    value_local = (
        projected[:, 2 * model_width :]
        .astype(jnp.bfloat16)
        .reshape(latents_here, tokens_here, model_width)
    )
    key_all, value_all = (
        lax.all_gather(key_local, "seq", axis=1, tiled=True),
        lax.all_gather(value_local, "seq", axis=1, tiled=True),
    )
    key_count = key_all.shape[1]
    key_heads = key_all.reshape(latents_here, key_count, head_count, head_size)
    value_heads = value_all.reshape(latents_here, key_count, head_count, head_size)
    scores = (
        jnp.einsum("bqhd,bkhd->bhqk", query, key_heads, preferred_element_type=jnp.float32)
        * score_scale
    )
    peak = jnp.max(scores, axis=-1, keepdims=True)
    log_total = jnp.log(jnp.sum(jnp.exp(scores - peak), axis=-1, keepdims=True)) + peak
    softmaxed = jnp.exp(scores - log_total)
    attended = jnp.einsum(
        "bhqk,bkhd->bqhd",
        softmaxed.astype(jnp.bfloat16),
        value_heads,
        preferred_element_type=jnp.float32,
    )
    attended = attended.astype(jnp.bfloat16).reshape(row_count, model_width)
    attention = (matmul(attended, full_proj) + bias_proj).reshape(
        latents_here, tokens_here, model_width
    )
    middle = inputs + gate_one * attention
    normed_two, norm_pull_two = jax.vjp(normalize, middle)
    second_rows = (
        (normed_two * (1.0 + scale_two) + shift_two)
        .astype(jnp.bfloat16)
        .reshape(row_count, model_width)
    )
    hidden = matmul(second_rows, full_fc1) + bias_fc1
    active, gelu_pull = jax.vjp(gelu_tanh, hidden)
    active_low = active.astype(jnp.bfloat16)
    branch = (matmul(active_low, full_fc2) + bias_fc2).reshape(
        latents_here, tokens_here, model_width
    )
    output = (middle + gate_two * branch).astype(jnp.bfloat16)
    regained = collect_back(w_ada, w_qkv, w_proj, w_fc1, w_fc2)
    full_ada, full_qkv, full_proj, full_fc1, full_fc2 = (
        regained[0],
        regained[1],
        regained[2],
        regained[3],
        regained[4],
    )
    grad_out = cotangent.astype(jnp.float32)
    gate_two_grad = jnp.sum(grad_out * branch, axis=1)
    branch_grad = (gate_two * grad_out).astype(jnp.bfloat16).reshape(row_count, model_width)
    fc2_bias_grad = jnp.sum(branch_grad.astype(jnp.float32), axis=0)
    fc2_grad = contract_rows(active_low, branch_grad)
    active_grad = contract_cols(branch_grad, full_fc2)
    hidden_grad = gelu_pull(active_grad)[0].astype(jnp.bfloat16)
    fc1_bias_grad = jnp.sum(hidden_grad.astype(jnp.float32), axis=0)
    fc1_grad = contract_rows(second_rows, hidden_grad)
    second_grad = contract_cols(hidden_grad, full_fc1).reshape(
        latents_here, tokens_here, model_width
    )
    shift_two_grad = jnp.sum(second_grad, axis=1)
    scale_two_grad = jnp.sum(second_grad * normed_two, axis=1)
    middle_grad = grad_out + norm_pull_two(second_grad * (1.0 + scale_two))[0]
    gate_one_grad = jnp.sum(middle_grad * attention, axis=1)
    attention_grad = (gate_one * middle_grad).astype(jnp.bfloat16).reshape(row_count, model_width)
    proj_bias_grad = jnp.sum(attention_grad.astype(jnp.float32), axis=0)
    proj_grad = contract_rows(attended, attention_grad)
    attended_grad = contract_cols(attention_grad, full_proj).astype(jnp.bfloat16)
    attended_grad = attended_grad.reshape(latents_here, tokens_here, head_count, head_size)
    scores = (
        jnp.einsum("bqhd,bkhd->bhqk", query, key_heads, preferred_element_type=jnp.float32)
        * score_scale
    )
    softmaxed = jnp.exp(scores - log_total)
    weight_grad = jnp.einsum(
        "bqhd,bkhd->bhqk", attended_grad, value_heads, preferred_element_type=jnp.float32
    )
    row_delta = jnp.sum(softmaxed * weight_grad, axis=-1, keepdims=True)
    score_grad = (softmaxed * (weight_grad - row_delta)).astype(jnp.bfloat16)
    query_grad = (
        jnp.einsum("bhqk,bkhd->bqhd", score_grad, key_heads, preferred_element_type=jnp.float32)
        * score_scale
    )
    key_grad = (
        jnp.einsum("bhqk,bqhd->bkhd", score_grad, query, preferred_element_type=jnp.float32)
        * score_scale
    )
    value_grad = jnp.einsum(
        "bhqk,bqhd->bkhd",
        softmaxed.astype(jnp.bfloat16),
        attended_grad,
        preferred_element_type=jnp.float32,
    )
    key_mine, value_mine = (
        lax.psum_scatter(
            key_grad.reshape(latents_here, key_count, model_width).astype(jnp.bfloat16),
            "seq",
            scatter_dimension=1,
            tiled=True,
        ).astype(jnp.float32),
        lax.psum_scatter(
            value_grad.reshape(latents_here, key_count, model_width).astype(jnp.bfloat16),
            "seq",
            scatter_dimension=1,
            tiled=True,
        ).astype(jnp.float32),
    )
    query_low = query_grad.astype(jnp.bfloat16).reshape(row_count, model_width)
    value_low = value_mine.astype(jnp.bfloat16).reshape(row_count, model_width)
    joint_grad = jnp.concatenate(
        [query_low, key_mine.astype(jnp.bfloat16).reshape(row_count, model_width), value_low],
        axis=-1,
    )
    query_bias_grad = jnp.sum(query_low.astype(jnp.float32), axis=0)
    value_bias_grad = jnp.sum(value_low.astype(jnp.float32), axis=0)
    qkv_grad = contract_rows(first_rows, joint_grad)
    first_grad = contract_cols(joint_grad, full_qkv).reshape(latents_here, tokens_here, model_width)
    shift_one_grad = jnp.sum(first_grad, axis=1)
    scale_one_grad = jnp.sum(first_grad * normed_one, axis=1)
    input_grad = middle_grad + norm_pull_one(first_grad * (1.0 + scale_one))[0]
    mods_grad = jnp.concatenate(
        [
            shift_one_grad,
            scale_one_grad,
            gate_one_grad,
            shift_two_grad,
            scale_two_grad,
            gate_two_grad,
        ],
        axis=-1,
    )
    mods_low = lax.psum(mods_grad.astype(jnp.bfloat16), "seq")
    leader = (lax.axis_index("seq") == 0).astype(jnp.float32)
    ada_grad = contract_rows(smooth_low, mods_low) * leader
    ada_bias_grad = jnp.sum(mods_low.astype(jnp.float32), axis=0) * leader
    smooth_grad = contract_cols(mods_low, full_ada)
    condition_grad = silu_pull(smooth_grad)[0]
    summed = (
        lax.psum_scatter(
            ada_grad.astype(jnp.bfloat16), "dp", scatter_dimension=0, tiled=True
        ).astype(jnp.float32),
        lax.psum_scatter(
            qkv_grad.astype(jnp.bfloat16), "dp", scatter_dimension=0, tiled=True
        ).astype(jnp.float32),
        lax.psum_scatter(
            proj_grad.astype(jnp.bfloat16), "dp", scatter_dimension=0, tiled=True
        ).astype(jnp.float32),
        lax.psum_scatter(
            fc1_grad.astype(jnp.bfloat16), "dp", scatter_dimension=0, tiled=True
        ).astype(jnp.float32),
        lax.psum_scatter(
            fc2_grad.astype(jnp.bfloat16), "dp", scatter_dimension=0, tiled=True
        ).astype(jnp.float32),
        lax.psum_scatter(
            ada_bias_grad.astype(jnp.bfloat16), "dp", scatter_dimension=0, tiled=True
        ).astype(jnp.float32),
        lax.psum_scatter(
            query_bias_grad.astype(jnp.bfloat16), "dp", scatter_dimension=0, tiled=True
        ).astype(jnp.float32),
        lax.psum_scatter(
            value_bias_grad.astype(jnp.bfloat16), "dp", scatter_dimension=0, tiled=True
        ).astype(jnp.float32),
        lax.psum_scatter(
            proj_bias_grad.astype(jnp.bfloat16), "dp", scatter_dimension=0, tiled=True
        ).astype(jnp.float32),
        lax.psum_scatter(
            fc1_bias_grad.astype(jnp.bfloat16), "dp", scatter_dimension=0, tiled=True
        ).astype(jnp.float32),
        lax.psum_scatter(
            fc2_bias_grad.astype(jnp.bfloat16), "dp", scatter_dimension=0, tiled=True
        ).astype(jnp.float32),
    )
    owned = (
        lax.psum_scatter(
            summed[0].astype(jnp.bfloat16), "seq", scatter_dimension=1, tiled=True
        ).astype(jnp.float32),
        lax.psum_scatter(
            summed[1].astype(jnp.bfloat16), "seq", scatter_dimension=1, tiled=True
        ).astype(jnp.float32),
        lax.psum_scatter(
            summed[2].astype(jnp.bfloat16), "seq", scatter_dimension=1, tiled=True
        ).astype(jnp.float32),
        lax.psum_scatter(
            summed[3].astype(jnp.bfloat16), "seq", scatter_dimension=1, tiled=True
        ).astype(jnp.float32),
        lax.psum_scatter(
            summed[4].astype(jnp.bfloat16), "seq", scatter_dimension=1, tiled=True
        ).astype(jnp.float32),
        lax.psum_scatter(
            summed[5].astype(jnp.bfloat16), "seq", scatter_dimension=0, tiled=True
        ).astype(jnp.float32),
        lax.psum_scatter(
            summed[6].astype(jnp.bfloat16), "seq", scatter_dimension=0, tiled=True
        ).astype(jnp.float32),
        lax.psum_scatter(
            summed[7].astype(jnp.bfloat16), "seq", scatter_dimension=0, tiled=True
        ).astype(jnp.float32),
        lax.psum_scatter(
            summed[8].astype(jnp.bfloat16), "seq", scatter_dimension=0, tiled=True
        ).astype(jnp.float32),
        lax.psum_scatter(
            summed[9].astype(jnp.bfloat16), "seq", scatter_dimension=0, tiled=True
        ).astype(jnp.float32),
        lax.psum_scatter(
            summed[10].astype(jnp.bfloat16), "seq", scatter_dimension=0, tiled=True
        ).astype(jnp.float32),
    )
    return (
        output,
        input_grad,
        condition_grad,
        owned[0],
        owned[5],
        owned[1],
        owned[6],
        owned[7],
        owned[2],
        owned[8],
        owned[3],
        owned[9],
        owned[4],
        owned[10],
    )


NT = (((1,), (1,)), ((), ()))
NN = (((1,), (0,)), ((), ()))


def product(left, right, dims):
    return lax.dot_general(left, right, dims, preferred_element_type=WIDE)


def flat(ref):
    value = ref[...]
    return value.reshape(value.shape[0] * value.shape[2], value.shape[3])


def attention_kernel(q_ref, k_ref, v_ref, o_ref, e_ref, r_ref, *, size, chunk):
    q, k, v = flat(q_ref), flat(k_ref), flat(v_ref)
    count = q.shape[0]
    scaled = q.astype(WIDE) * (LOG2E * size**-0.5)
    high = scaled.astype(LOW)
    rest = (scaled - high.astype(WIDE)).astype(LOW)
    v_t = v.astype(WIDE).T.astype(LOW)
    ones = jnp.ones((16, count), LOW)
    outs, inverses = [], []
    for head in range(q.shape[1] // size):
        cols = slice(head * size, (head + 1) * size)
        keys = jnp.concatenate([k[:, cols], k[:, cols]], 1)
        queries = jnp.concatenate([high[:, cols], rest[:, cols]], 1)
        values = jnp.concatenate([v_t[cols], ones], 0)
        out_parts, inverse_parts = [], []
        for at in range(0, count, chunk):
            scores = product(keys, queries[at : at + chunk], NT)
            peak = jnp.max(scores, axis=0, keepdims=True)
            weights = jnp.exp2(scores - peak).astype(LOW)
            e_ref[0, 0, head, :, at : at + chunk] = weights
            summed = product(values, weights, NN)
            inverse = 1.0 / summed[size : size + 1]
            out_parts.append(summed[:size] * inverse)
            inverse_parts.append(inverse)
        outs.append(jnp.concatenate(out_parts, 1))
        inverses.append(jnp.concatenate(inverse_parts, 1))
    o_ref[...] = jnp.concatenate(outs, 0).T.astype(LOW).reshape(o_ref.shape)
    r_ref[0, 0] = jnp.concatenate(inverses, 0)


def attention_back_kernel(
    q_ref, k_ref, v_ref, o_ref, do_ref, e_ref, r_ref, dq_ref, dk_ref, dv_ref, *, size
):
    q, k, v = flat(q_ref), flat(k_ref), flat(v_ref)
    do, o = flat(do_ref).astype(WIDE), flat(o_ref).astype(WIDE)
    scale = size**-0.5
    inverse = r_ref[0, 0]
    prod_t = (do * o).T
    do_t = do.T
    k_t = (k.astype(WIDE) * scale).T.astype(LOW)
    q_scaled = (q.astype(WIDE) * scale).astype(LOW)
    dqs, dks, dvs = [], [], []
    for head in range(q.shape[1] // size):
        cols = slice(head * size, (head + 1) * size)
        inv = inverse[head : head + 1]
        grad_t = do_t[cols] * inv
        delta = jnp.sum(prod_t[cols], axis=0, keepdims=True) * inv
        weights = e_ref[0, 0, head]
        da = product(v[:, cols], grad_t.astype(LOW), NN)
        ds = weights * (da - delta).astype(LOW)
        dqs.append(product(k_t[cols], ds, NN))
        dks.append(product(ds, q_scaled[:, cols], NN))
        dvs.append(product(weights, grad_t.T.astype(LOW), NN))
    dq_ref[...] = jnp.concatenate(dqs, 0).T.astype(LOW).reshape(dq_ref.shape)
    dk_ref[...] = jnp.concatenate(dks, 1).astype(LOW).reshape(dk_ref.shape)
    dv_ref[...] = jnp.concatenate(dvs, 1).astype(LOW).reshape(dv_ref.shape)


PARAMS = pltpu.CompilerParams(vmem_limit_bytes=56 << 20)


def attention_blocks(half, tokens, width):
    def columns(base):
        return pl.BlockSpec((half, 1, tokens, width), lambda latent, pair: (0, latent, 0, base + pair))

    return columns


def attention_fore(qkv):
    half, latents, tokens, triple = qkv.shape
    model = triple // 3
    size = model // HEADS
    per = 128 // size
    pairs = HEADS // per
    count = half * tokens
    columns = attention_blocks(half, tokens, 128)
    flops = 4 * latents * HEADS * count * count * 128
    return pl.pallas_call(
        functools.partial(attention_kernel, size=size, chunk=count),
        grid=(latents, pairs),
        in_specs=[columns(0), columns(pairs), columns(2 * pairs)],
        out_specs=[
            columns(0),
            pl.BlockSpec((1, 1, per, count, count), lambda latent, pair: (latent, pair, 0, 0, 0)),
            pl.BlockSpec((1, 1, per, count), lambda latent, pair: (latent, pair, 0, 0)),
        ],
        out_shape=[
            jax.ShapeDtypeStruct((half, latents, tokens, model), LOW),
            jax.ShapeDtypeStruct((latents, pairs, per, count, count), LOW),
            jax.ShapeDtypeStruct((latents, pairs, per, count), WIDE),
        ],
        compiler_params=PARAMS,
        cost_estimate=pl.CostEstimate(
            flops=flops, bytes_accessed=90 << 20, transcendentals=latents * HEADS * count * count
        ),
        name="attention_fore",
    )(qkv, qkv, qkv)


def attention_back(qkv, attended, attended_grad, weights, inverse):
    half, latents, tokens, triple = qkv.shape
    model = triple // 3
    size = model // HEADS
    per = 128 // size
    pairs = HEADS // per
    count = half * tokens
    columns = attention_blocks(half, tokens, 128)
    flops = 8 * latents * HEADS * count * count * 128
    grads = jax.ShapeDtypeStruct((half, latents, tokens, model), LOW)
    return pl.pallas_call(
        functools.partial(attention_back_kernel, size=size),
        grid=(latents, pairs),
        in_specs=[
            columns(0),
            columns(pairs),
            columns(2 * pairs),
            columns(0),
            columns(0),
            pl.BlockSpec((1, 1, per, count, count), lambda latent, pair: (latent, pair, 0, 0, 0)),
            pl.BlockSpec((1, 1, per, count), lambda latent, pair: (latent, pair, 0, 0)),
        ],
        out_specs=[columns(0)] * 3,
        out_shape=[grads] * 3,
        compiler_params=PARAMS,
        cost_estimate=pl.CostEstimate(flops=flops, bytes_accessed=100 << 20, transcendentals=0),
        name="attention_back",
    )(qkv, qkv, qkv, attended, attended_grad, weights, inverse)


SIX = 6


def norm_parts(rows):
    centre = rows - jnp.mean(rows, axis=1, keepdims=True)
    inverse = lax.rsqrt(jnp.mean(centre * centre, axis=1, keepdims=True) + 1e-06)
    return centre * inverse, inverse


def norm_back(grad, normed, inverse):
    mean = jnp.mean(grad, axis=1, keepdims=True)
    along = jnp.mean(grad * normed, axis=1, keepdims=True)
    return (grad - mean - normed * along) * inverse


def down_sum(value):
    return jnp.sum(value, axis=0, keepdims=True)


def accumulate(ref, value, start):
    @pl.when(start)
    def _():
        ref[...] = value.reshape(ref.shape)

    @pl.when(jnp.logical_not(start))
    def _():
        ref[...] += value.reshape(ref.shape)


def first_of_latent():
    return (pl.program_id(1) == 0) & (pl.program_id(2) == 0)


def first_of_all():
    return (pl.program_id(0) == 0) & first_of_latent()


class Bundle:
    def __init__(self, ref, hidden):
        self.ref = ref
        self.dp, rows, self.width = ref.shape
        self.count = hidden // self.width
        self.high = self.width // self.dp
        self.low = hidden // self.dp

    def take(self, places, rows):
        return self.ref[places, rows, :].reshape(self.width, self.width)

    def fc1(self, block):
        return self.take(slice(0, self.dp), slice(block * self.high, (block + 1) * self.high))

    def proj(self):
        return self.fc1(self.count)

    def fc2(self, block):
        start = (self.count + 1) * self.high
        per = self.dp // self.count
        return self.take(slice(block * per, (block + 1) * per), slice(start, start + self.low))


def project_kernel(x_ref, mods_ref, w_ref, bias_ref, first_ref, qkv_ref):
    mods = mods_ref[0]
    normed, _ = norm_parts(x_ref[0, 0].astype(WIDE))
    first = (normed * (1.0 + mods[1:2]) + mods[0:1]).astype(LOW)
    first_ref[0, 0] = first
    model = first.shape[1]
    for at in range(0, 3 * model, model):
        cols = slice(at, at + model)
        qkv_ref[0, 0, :, cols] = (product(first, w_ref[:, cols], NN) + bias_ref[:, cols]).astype(LOW)


def forward_kernel(
    x_ref, o_ref, dy_ref, mods_ref, bundle_ref, b_proj_ref, b1_ref, b2_ref,
    out_ref, second_ref, active_ref, slope_ref, attention_ref, middle_ref, dm_ref, gate_ref,
):
    mods = mods_ref[0]
    bundle = Bundle(bundle_ref, b1_ref.shape[1])
    attention = product(o_ref[0, 0], bundle.proj(), NN) + b_proj_ref[...]
    attention_ref[0, 0] = attention.astype(LOW)
    middle = x_ref[0, 0].astype(WIDE) + mods[2:3] * attention
    middle_ref[0, 0] = middle
    normed, _ = norm_parts(middle)
    second = (normed * (1.0 + mods[4:5]) + mods[3:4]).astype(LOW)
    second_ref[0, 0] = second
    branch = b2_ref[...]
    width = second.shape[1]
    for block in range(bundle.count):
        cols = slice(block * width, (block + 1) * width)
        hidden = product(second, bundle.fc1(block), NN) + b1_ref[:, cols]
        square = hidden * hidden
        bend = jnp.tanh(hidden * (0.7978845608028654 + 0.035677408136300125 * square))
        half = 0.5 + 0.5 * bend
        active = (hidden * half).astype(LOW)
        steep = 0.7978845608028654 + 0.10703222440890037 * square
        slope = half + (0.5 * hidden) * (1.0 - bend * bend) * steep
        active_ref[0, 0, :, cols] = active
        slope_ref[0, 0, :, cols] = slope.astype(LOW)
        branch = branch + product(active, bundle.fc2(block), NN)
    out_ref[0, 0] = (middle + mods[5:6] * branch).astype(LOW)
    dy = dy_ref[0, 0].astype(WIDE)
    dm_ref[0, 0] = (mods[5:6] * dy).astype(LOW)
    accumulate(gate_ref, down_sum(dy * branch), first_of_latent())


def backward_kernel(
    dy_ref, dm_ref, slope_ref, middle_ref, attention_ref, mods_ref, bundle_ref,
    dh_ref, dmiddle_ref, dattention_ref, do_ref, sums_ref, b1_ref, b2_ref, b_proj_ref,
):
    mods = mods_ref[0]
    dm = dm_ref[0, 0]
    width = dm.shape[1]
    start = first_of_all()
    dsecond = None
    bundle = Bundle(bundle_ref, b1_ref.shape[1])
    for block in range(bundle.count):
        cols = slice(block * width, (block + 1) * width)
        dh = (product(dm, bundle.fc2(block), NT) * slope_ref[0, 0, :, cols].astype(WIDE)).astype(LOW)
        dh_ref[0, 0, :, cols] = dh
        accumulate(b1_ref.at[:, cols], down_sum(dh.astype(WIDE)), start)
        part = product(dh, bundle.fc1(block), NT)
        dsecond = part if dsecond is None else dsecond + part
    normed, inverse = norm_parts(middle_ref[0, 0])
    dmiddle = dy_ref[0, 0].astype(WIDE) + norm_back(dsecond * (1.0 + mods[4:5]), normed, inverse)
    dmiddle_ref[0, 0] = dmiddle
    dattention = (mods[2:3] * dmiddle).astype(LOW)
    dattention_ref[0, 0] = dattention
    do_ref[0, 0] = product(dattention, bundle.proj(), NT).astype(LOW)
    sums = jnp.concatenate(
        [
            down_sum(dmiddle * attention_ref[0, 0].astype(WIDE)),
            down_sum(dsecond),
            down_sum(dsecond * normed),
        ],
        axis=0,
    )
    accumulate(sums_ref, sums, first_of_latent())
    accumulate(b2_ref, down_sum(dm.astype(WIDE)), start)
    accumulate(b_proj_ref, down_sum(dattention.astype(WIDE)), start)


def project_back_kernel(
    dq_ref, dk_ref, dv_ref, x_ref, dmiddle_ref, mods_ref, w_ref, dx_ref, sums_ref, bq_ref, bv_ref
):
    mods = mods_ref[0]
    model = x_ref.shape[3]
    grads = [dq_ref[0, 0], dk_ref[0, 0], dv_ref[0, 0]]
    dfirst = sum(
        product(grad, w_ref[:, i * model : (i + 1) * model], NT) for i, grad in enumerate(grads)
    )
    normed, inverse = norm_parts(x_ref[0, 0].astype(WIDE))
    dx_ref[0, 0] = dmiddle_ref[0, 0] + norm_back(dfirst * (1.0 + mods[1:2]), normed, inverse)
    sums = jnp.concatenate([down_sum(dfirst), down_sum(dfirst * normed)], axis=0)
    accumulate(sums_ref, sums, first_of_latent())
    start = first_of_all()
    accumulate(bq_ref, down_sum(grads[0].astype(WIDE)), start)
    accumulate(bv_ref, down_sum(grads[2].astype(WIDE)), start)


def row_call(kernel, like, operands, results, flops, name, span):
    half, latents, tokens, _ = like.shape
    span = min(span, tokens)

    def spec(shape, kind):
        if kind == "rows":
            return pl.BlockSpec((1, 1, span, shape[3]), lambda l, h, i: (h, l, i, 0))
        if kind == "latent":
            return pl.BlockSpec((1,) + shape[1:], lambda l, h, i: (l,) + (0,) * (len(shape) - 1))
        if kind == "whole":
            zeros = (0,) * len(shape)
            return pl.BlockSpec(shape, lambda l, h, i: zeros, pipeline_mode=pl.Buffered(1))
        width, index = kind
        return pl.BlockSpec(
            (shape[0], width), lambda l, h, i: (0, index), pipeline_mode=pl.Buffered(1)
        )

    def out_spec(shape, kind):
        if kind == "all":
            return pl.BlockSpec(shape, lambda l, h, i: (0, 0))
        return spec(shape, kind)

    return pl.pallas_call(
        kernel,
        grid=(latents, half, tokens // span),
        in_specs=[spec(a.shape, kind) for a, kind in operands],
        out_specs=[out_spec(shape, kind) for shape, _, kind in results],
        out_shape=[jax.ShapeDtypeStruct(shape, dtype) for shape, dtype, _ in results],
        compiler_params=PARAMS,
        cost_estimate=pl.CostEstimate(flops=flops, bytes_accessed=64 << 20, transcendentals=0),
        name=name,
    )(*(a for a, _ in operands))


class Wires:
    def __init__(self, dp):
        self.depth = dp // 4
        index = lax.axis_index("dp")
        self.z, self.y, self.core = index // 4, (index // 2) % 2, index % 2
        self.x = lax.axis_index("seq")
        self.places = [(z, y, c) for z in range(self.depth) for y in range(2) for c in range(2)]

    def across(self, value):
        return lax.ppermute(value, "seq", [(0, 1), (1, 0)])

    def dp_step(self, value, move):
        pairs = []
        for z, y, c in self.places:
            to_z, to_y, to_c = move(z, y, c)
            pairs.append(((z * 2 + y) * 2 + c, (to_z * 2 + to_y) * 2 + to_c))
        return lax.ppermute(value, "dp", pairs)

    def distances(self):
        steps, distance = [], self.depth // 2
        while distance:
            steps.append(distance)
            distance //= 2
        return steps

    def bit(self, distance):
        return (self.z // distance) % 2

    def mirror(self, value, distance):
        return self.dp_step(value, lambda z, y, c: (z ^ distance, y, c))

    def beside(self, value):
        return self.dp_step(value, lambda z, y, c: (z, 1 - y, c))

    def twin(self, value):
        return self.dp_step(value, lambda z, y, c: (z, y, 1 - c))


def pick(value, index, axis):
    return lax.dynamic_index_in_dim(value, index, axis, keepdims=False)


def order_two(mine, other, index, axis, fresh=False):
    if fresh:
        mine, other = mine[:, None], other[:, None]
        both = order_two(mine, other, index, 1)
        return both.reshape((-1,) + both.shape[2:])
    return jnp.where(
        index == 0,
        jnp.concatenate([mine, other], axis),
        jnp.concatenate([other, mine], axis),
    )


def gather_small(wires, value):
    held = value[None]
    for distance in wires.distances():
        held = order_two(held, wires.mirror(held, distance), wires.bit(distance), 0, True)
    held = order_two(held, wires.beside(held), wires.y, 0, True)
    held = order_two(held, wires.twin(held), wires.core, 0, True)
    return held


def sum_small(wires, value):
    held = value.reshape((wires.depth, 2, 2) + value.shape[1:])
    held = pick(held, wires.core, 2) + wires.twin(pick(held, 1 - wires.core, 2))
    held = pick(held, wires.y, 1) + wires.beside(pick(held, 1 - wires.y, 1))
    return sum_line(wires, held, 1)


def sum_line(wires, held, nearest):
    distances = [distance for distance in wires.distances() if distance >= nearest]
    held = held.reshape((2,) * len(distances) + held.shape[1:])
    for place, distance in reversed(list(enumerate(distances))):
        bit = wires.bit(distance)
        held = pick(held, bit, place) + wires.mirror(pick(held, 1 - bit, place), distance)
    return held


def add_low(left, right):
    return (left.astype(WIDE) + right.astype(WIDE)).astype(LOW)


def split_columns(wires, *wholes):
    halves = [whole.reshape(whole.shape[0], 2, whole.shape[1] // 2) for whole in wholes]
    theirs = wires.across(jnp.concatenate([pick(half, 1 - wires.x, 1) for half in halves], axis=1))
    ends = [sum(half.shape[2] for half in halves[:i]) for i in range(len(halves))]
    return [
        pick(half, wires.x, 1).astype(WIDE) + theirs[:, end : end + half.shape[2]].astype(WIDE)
        for half, end in zip(halves, ends)
    ]


def fast_body(
    dp,
    tokens,
    condition,
    w_ada,
    b_ada,
    w_qkv,
    q_bias,
    v_bias,
    w_proj,
    b_proj,
    w_fc1,
    b_fc1,
    w_fc2,
    b_fc2,
    cotangent,
):
    wires = Wires(dp)
    group, tokens_here, model = tokens.shape
    mine = group // 2
    rows = group * tokens_here
    x, z_y_c = wires.x, lax.axis_index("dp")

    def swap(value):
        ours = lax.dynamic_slice_in_dim(value, x * mine, mine, 0)
        theirs = lax.dynamic_slice_in_dim(value, (1 - x) * mine, mine, 0)
        return ours, wires.across(theirs)

    def swap_back(value, theirs):
        return order_two(value[0], theirs.astype(value.dtype), x, 0)

    packed = jnp.concatenate([w_qkv, w_proj, w_fc1], axis=1)
    theirs = wires.across(packed)
    cuts = [w_qkv.shape[1], w_qkv.shape[1] + w_proj.shape[1]]
    own_qkv, own_proj, own_fc1 = (
        order_two(a, b, x, 1) for a, b in zip(jnp.split(packed, cuts, 1), jnp.split(theirs, cuts, 1))
    )
    own_fc2 = order_two(w_fc2, wires.across(w_fc2), x, 1)
    full_qkv = lax.all_gather(own_qkv, "dp", axis=0, tiled=True)
    blocks = jnp.split(own_fc1, own_fc1.shape[1] // model, 1) + [own_proj, own_fc2]
    bundle = lax.all_gather(jnp.concatenate(blocks, axis=0), "dp", axis=0, tiled=False)
    tokens, own_fc2 = lax.optimization_barrier((tokens, own_fc2))
    tokens_mine, tokens_across = swap(tokens)

    vectors = (q_bias, v_bias, b_proj, b_fc1, b_fc2, b_ada)
    sizes = [v.shape[0] for v in vectors]
    offsets = [sum(sizes[:i]) for i in range(len(sizes))]
    biases = jnp.concatenate(vectors)[None]
    biases = order_two(biases, wires.across(biases), x, 0)
    smooth, silu_pull = jax.vjp(jax.nn.silu, condition)
    smooth_low = smooth.astype(LOW)
    vector = jnp.concatenate([smooth_low.reshape(-1), biases.reshape(-1)])
    vector = gather_small(wires, vector)
    joined = vector[:, group * model :].reshape(2 * dp, -1)
    bias_query, bias_value, bias_proj, bias_fc1, bias_fc2, bias_ada = (
        joined[:, o : o + n].reshape(-1).astype(WIDE) for o, n in zip(offsets, sizes)
    )

    smooth_all = vector[:, : group * model].reshape(dp * group, model)
    ada_rows = w_ada.shape[0]
    smooth_mine = lax.dynamic_slice_in_dim(smooth_all, z_y_c * ada_rows, ada_rows, 1)
    partial = matmul(smooth_mine, w_ada)
    half_mods = sum_small(wires, partial.reshape(dp, group, -1))
    tokens_across, half_mods = lax.optimization_barrier((tokens_across, half_mods))
    tokens_two = jnp.stack([tokens_mine, tokens_across])
    ours, theirs = swap(half_mods)
    mods = order_two(ours, theirs, x, 1) + bias_ada
    mods = mods.reshape(mine, SIX, model)
    hidden_width = dp * w_fc2.shape[0]
    rows4 = lambda width: (2, mine, tokens_here, width)
    bias_row = jnp.concatenate([bias_query, jnp.zeros_like(bias_query), bias_value])[None]
    first, qkv = row_call(
        project_kernel,
        tokens_two,
        [
            (tokens_two, "rows"),
            (mods, "latent"),
            (full_qkv, (3 * model, 0)),
            (bias_row, (3 * model, 0)),
        ],
        [(rows4(model), LOW, "rows"), (rows4(3 * model), LOW, "rows")],
        6 * rows * model * model,
        "project",
        512,
    )
    cotangent, w_ada, qkv = lax.optimization_barrier((cotangent, w_ada, qkv))
    ada_across = wires.across(w_ada)
    ours, theirs = swap(cotangent)
    attended, weights, inverse = attention_fore(qkv)
    ada_across, theirs, attended = lax.optimization_barrier((ada_across, theirs, attended))
    both_ada = order_two(w_ada, ada_across, x, 1)
    cotangent_two = jnp.stack([ours, theirs])
    (output, second, active, slope, attention, middle, branch_grad, gate_two_grad) = row_call(
        forward_kernel,
        tokens_two,
        [
            (tokens_two, "rows"),
            (attended, "rows"),
            (cotangent_two, "rows"),
            (mods, "latent"),
            (bundle, "whole"),
            (bias_proj[None], (model, 0)),
            (bias_fc1[None], (hidden_width, 0)),
            (bias_fc2[None], (model, 0)),
        ],
        [
            (rows4(model), LOW, "rows"),
            (rows4(model), LOW, "rows"),
            (rows4(hidden_width), LOW, "rows"),
            (rows4(hidden_width), LOW, "rows"),
            (rows4(model), LOW, "rows"),
            (rows4(model), WIDE, "rows"),
            (rows4(model), LOW, "rows"),
            ((mine, 1, model), WIDE, "latent"),
        ],
        2 * rows * model * (model + 2 * hidden_width),
        "forward",
        256,
    )

    def flat_rows(value):
        return value.reshape(rows, value.shape[-1])

    output_across = wires.across(output[1])
    fc2_grad = contract_rows(flat_rows(active), flat_rows(branch_grad)).astype(LOW)
    branch_grad, fc2_grad = lax.optimization_barrier((branch_grad, fc2_grad))
    fc2_rows = lax.psum_scatter(fc2_grad, "dp", scatter_dimension=0, tiled=True)
    (
        hidden_grad,
        middle_grad,
        attention_grad,
        attended_grad,
        middle_sums,
        fc1_bias_grad,
        fc2_bias_grad,
        proj_bias_grad,
    ) = row_call(
        backward_kernel,
        tokens_two,
        [
            (cotangent_two, "rows"),
            (branch_grad, "rows"),
            (slope, "rows"),
            (middle, "rows"),
            (attention, "rows"),
            (mods, "latent"),
            (bundle, "whole"),
        ],
        [
            (rows4(hidden_width), LOW, "rows"),
            (rows4(model), WIDE, "rows"),
            (rows4(model), LOW, "rows"),
            (rows4(model), LOW, "rows"),
            ((mine, 3, model), WIDE, "latent"),
            ((1, hidden_width), WIDE, "all"),
            ((1, model), WIDE, "all"),
            ((1, model), WIDE, "all"),
        ],
        2 * rows * model * (model + 2 * hidden_width),
        "backward",
        256,
    )
    fc1_grad = contract_rows(flat_rows(second), flat_rows(hidden_grad)).astype(LOW)
    attention_grad, fc1_grad = lax.optimization_barrier((attention_grad, fc1_grad))
    fc1_rows = lax.psum_scatter(fc1_grad, "dp", scatter_dimension=0, tiled=True)
    proj_grad = contract_rows(flat_rows(attended), flat_rows(attention_grad)).astype(LOW)
    attended_grad, proj_grad, fc2_rows = lax.optimization_barrier((attended_grad, proj_grad, fc2_rows))
    (fc2_grad,) = split_columns(wires, fc2_rows)
    dq, dk, dv = attention_back(qkv, attended, attended_grad, weights, inverse)
    dq, output_across = lax.optimization_barrier((dq, output_across))
    output = swap_back(output, output_across)
    joint = jnp.concatenate([flat_rows(d) for d in (dq, dk, dv)], axis=-1)
    qkv_grad = contract_rows(flat_rows(first), joint).astype(LOW)
    last_grad = jnp.concatenate([qkv_grad, proj_grad], axis=1)
    last_grad = last_grad.reshape((wires.depth, 2, 2, -1) + last_grad.shape[1:])
    kept = pick(last_grad, wires.core, 2)
    twins = wires.twin(pick(last_grad, 1 - wires.core, 2))
    dk, twins, fc1_rows = lax.optimization_barrier((dk, twins, fc1_rows))
    (fc1_grad,) = split_columns(wires, fc1_rows)
    kept = add_low(kept, twins)
    left, right = jnp.split(kept, 2, axis=3)
    right = right.reshape((wires.depth // 2, 2) + right.shape[1:])
    left_keep, left_across = pick(left, wires.y, 1), wires.beside(pick(left, 1 - wires.y, 1))
    low_bit = wires.bit(1)
    right_keep, right_across = pick(right, low_bit, 1), wires.mirror(pick(right, 1 - low_bit, 1), 1)
    input_grad, first_sums, query_bias_grad, value_bias_grad = row_call(
        project_back_kernel,
        tokens_two,
        [
            (dq, "rows"),
            (dk, "rows"),
            (dv, "rows"),
            (tokens_two, "rows"),
            (middle_grad, "rows"),
            (mods, "latent"),
            (full_qkv, (3 * model, 0)),
        ],
        [
            (rows4(model), WIDE, "rows"),
            ((mine, 2, model), WIDE, "latent"),
            ((1, model), WIDE, "all"),
            ((1, model), WIDE, "all"),
        ],
        6 * rows * model * model,
        "project_back",
        512,
    )
    input_grad, left_across, right_across = lax.optimization_barrier(
        (input_grad, left_across, right_across)
    )
    left, right = add_low(left_keep, left_across), add_low(right_keep, right_across)

    mods_grad = jnp.concatenate([first_sums, middle_sums, gate_two_grad], axis=1).astype(LOW)
    mods_grad = mods_grad.reshape(mine, SIX * model)
    sums = (query_bias_grad, value_bias_grad, proj_bias_grad, fc1_bias_grad, fc2_bias_grad)
    bias_sums = jnp.concatenate([v.reshape(2 * dp, -1) for v in sums], axis=1).reshape(dp, 2, -1)
    bias_sums = pick(bias_sums, x, 1) + wires.across(pick(bias_sums, 1 - x, 1))
    group_grad = order_two(mods_grad, wires.across(mods_grad), x, 0)
    input_grad, group_grad, bias_sums = lax.optimization_barrier((input_grad, group_grad, bias_sums))
    input_across = wires.across(input_grad[1].astype(LOW))
    left = sum_line(wires, left, 1)
    right = add_low(pick(right, wires.y, 1), wires.beside(pick(right, 1 - wires.y, 1)))
    right = sum_line(wires, right, 2)
    last_rows = jnp.concatenate([left, right], axis=1)
    qkv_grad, proj_grad = split_columns(wires, *jnp.split(last_rows, [3 * model], axis=1))
    owned = sum_small(wires, bias_sums)
    all_grad = gather_small(wires, group_grad).reshape(dp * group, -1)
    all_grad, input_across = lax.optimization_barrier((all_grad, input_across))
    input_grad = swap_back(input_grad, input_across)
    half_grad = lax.dynamic_slice_in_dim(all_grad, x * 3 * model, 3 * model, 1)
    ada_grad = contract_rows(smooth_mine, half_grad)
    ada_bias_grad = lax.dynamic_slice_in_dim(
        jnp.sum(all_grad.astype(WIDE), axis=0), (z_y_c * 2 + x) * b_ada.shape[0], b_ada.shape[0], 0
    )
    smooth_part = contract_cols(all_grad, both_ada)
    spread = lax.all_to_all(
        smooth_part.reshape(dp, group, ada_rows), "dp", 0, 0, tiled=False
    )
    smooth_grad = jnp.swapaxes(spread, 0, 1).reshape(group, model)
    condition_grad = silu_pull(smooth_grad)[0]

    bias_grads = [owned[o : o + n] for o, n in zip(offsets, sizes[:5])]
    return (
        output,
        input_grad,
        condition_grad,
        ada_grad,
        ada_bias_grad,
        qkv_grad,
        bias_grads[0],
        bias_grads[1],
        proj_grad,
        bias_grads[2],
        fc1_grad,
        bias_grads[3],
        fc2_grad,
        bias_grads[4],
    )


def solution(mesh):
    sizes = dict(mesh.shape)

    def body(tokens, *others):
        split = sizes["seq"] == 2 and sizes["dp"] % 4 == 0 and tokens.shape[0] % 2 == 0
        if split:
            return fast_body(sizes["dp"], tokens, *others)
        return general_body(tokens, *others)

    return jax.shard_map(
        body,
        mesh=mesh,
        in_specs=(
            P("dp", "seq", None),
            P("dp", None),
            P("dp", "seq"),
            P(("dp", "seq")),
            P("dp", "seq"),
            P(("dp", "seq")),
            P(("dp", "seq")),
            P("dp", "seq"),
            P(("dp", "seq")),
            P("dp", "seq"),
            P(("dp", "seq")),
            P("dp", "seq"),
            P(("dp", "seq")),
            P("dp", "seq", None),
        ),
        out_specs=(
            P("dp", "seq", None),
            P("dp", "seq", None),
            P("dp", None),
            P("dp", "seq"),
            P(("dp", "seq")),
            P("dp", "seq"),
            P(("dp", "seq")),
            P(("dp", "seq")),
            P("dp", "seq"),
            P(("dp", "seq")),
            P("dp", "seq"),
            P(("dp", "seq")),
            P("dp", "seq"),
            P(("dp", "seq")),
        ),
        check_vma=False,
    )
```

```python
import functools

import jax
import jax.numpy as jnp
from jax import lax
from jax.experimental import pallas as pl
from jax.experimental.pallas import tpu as pltpu
from jax.sharding import PartitionSpec as P

HEADS = 16
LOW = jnp.bfloat16
WIDE = jnp.float32
LOG2E = 1.4426950408889634


def normalize(rows):
    centre = rows - jnp.mean(rows, axis=-1, keepdims=True)
    return centre * lax.rsqrt(jnp.mean(centre * centre, axis=-1, keepdims=True) + 1e-06)


def gelu_tanh(value):
    return jax.nn.gelu(value, approximate=True)


def matmul(left, right):
    return jnp.dot(left, right, preferred_element_type=jnp.float32)


def contract_rows(left, right):
    return lax.dot_general(
        left, right, (((0,), (0,)), ((), ())), preferred_element_type=jnp.float32
    )


def contract_cols(left, right):
    return lax.dot_general(
        left, right, (((1,), (1,)), ((), ())), preferred_element_type=jnp.float32
    )


def collect_fore(w_ada, w_qkv, w_proj, w_fc1, w_fc2, b_ada, q_bias, v_bias, b_proj, b_fc1, b_fc2):
    inner = (
        lax.all_gather(w_ada, "seq", axis=1, tiled=True),
        lax.all_gather(w_qkv, "seq", axis=1, tiled=True),
        lax.all_gather(w_proj, "seq", axis=1, tiled=True),
        lax.all_gather(w_fc1, "seq", axis=1, tiled=True),
        lax.all_gather(w_fc2, "seq", axis=1, tiled=True),
        lax.all_gather(b_ada, "seq", axis=0, tiled=True),
        lax.all_gather(q_bias, "seq", axis=0, tiled=True),
        lax.all_gather(v_bias, "seq", axis=0, tiled=True),
        lax.all_gather(b_proj, "seq", axis=0, tiled=True),
        lax.all_gather(b_fc1, "seq", axis=0, tiled=True),
        lax.all_gather(b_fc2, "seq", axis=0, tiled=True),
    )
    return (
        lax.all_gather(inner[0], "dp", axis=0, tiled=True),
        lax.all_gather(inner[1], "dp", axis=0, tiled=True),
        lax.all_gather(inner[2], "dp", axis=0, tiled=True),
        lax.all_gather(inner[3], "dp", axis=0, tiled=True),
        lax.all_gather(inner[4], "dp", axis=0, tiled=True),
        lax.all_gather(inner[5], "dp", axis=0, tiled=True),
        lax.all_gather(inner[6], "dp", axis=0, tiled=True),
        lax.all_gather(inner[7], "dp", axis=0, tiled=True),
        lax.all_gather(inner[8], "dp", axis=0, tiled=True),
        lax.all_gather(inner[9], "dp", axis=0, tiled=True),
        lax.all_gather(inner[10], "dp", axis=0, tiled=True),
    )


def collect_back(w_ada, w_qkv, w_proj, w_fc1, w_fc2):
    inner = (
        lax.all_gather(w_ada, "seq", axis=1, tiled=True),
        lax.all_gather(w_qkv, "seq", axis=1, tiled=True),
        lax.all_gather(w_proj, "seq", axis=1, tiled=True),
        lax.all_gather(w_fc1, "seq", axis=1, tiled=True),
        lax.all_gather(w_fc2, "seq", axis=1, tiled=True),
    )
    return (
        lax.all_gather(inner[0], "dp", axis=0, tiled=True),
        lax.all_gather(inner[1], "dp", axis=0, tiled=True),
        lax.all_gather(inner[2], "dp", axis=0, tiled=True),
        lax.all_gather(inner[3], "dp", axis=0, tiled=True),
        lax.all_gather(inner[4], "dp", axis=0, tiled=True),
    )


def general_body(
    tokens,
    condition,
    w_ada,
    b_ada,
    w_qkv,
    q_bias,
    v_bias,
    w_proj,
    b_proj,
    w_fc1,
    b_fc1,
    w_fc2,
    b_fc2,
    cotangent,
):
    latents_here, tokens_here, model_width = tokens.shape
    head_count = HEADS
    head_size = model_width // head_count
    score_scale = head_size ** (-0.5)
    row_count = latents_here * tokens_here
    gathered = collect_fore(
        w_ada, w_qkv, w_proj, w_fc1, w_fc2, b_ada, q_bias, v_bias, b_proj, b_fc1, b_fc2
    )
    full_ada, full_qkv, full_proj, full_fc1, full_fc2 = (
        gathered[0],
        gathered[1],
        gathered[2],
        gathered[3],
        gathered[4],
    )
    bias_ada = gathered[5].astype(jnp.float32)
    bias_query = gathered[6].astype(jnp.float32)
    bias_value = gathered[7].astype(jnp.float32)
    bias_proj = gathered[8].astype(jnp.float32)
    bias_fc1 = gathered[9].astype(jnp.float32)
    bias_fc2 = gathered[10].astype(jnp.float32)
    inputs = tokens.astype(jnp.float32)
    smooth, silu_pull = jax.vjp(jax.nn.silu, condition)
    smooth_low = smooth.astype(jnp.bfloat16)
    mods = matmul(smooth_low, full_ada) + bias_ada
    pieces = [mods[:, None, index * model_width : (index + 1) * model_width] for index in range(6)]
    shift_one, scale_one, gate_one, shift_two, scale_two, gate_two = pieces
    normed_one, norm_pull_one = jax.vjp(normalize, inputs)
    first_rows = (
        (normed_one * (1.0 + scale_one) + shift_one)
        .astype(jnp.bfloat16)
        .reshape(row_count, model_width)
    )
    bias_row = jnp.concatenate([bias_query, jnp.zeros_like(bias_query), bias_value])
    projected = matmul(first_rows, full_qkv) + bias_row
    query = (
        projected[:, :model_width]
        .astype(jnp.bfloat16)
        .reshape(latents_here, tokens_here, head_count, head_size)
    )
    key_local = (
        projected[:, model_width : 2 * model_width]
        .astype(jnp.bfloat16)
        .reshape(latents_here, tokens_here, model_width)
    )
    value_local = (
        projected[:, 2 * model_width :]
        .astype(jnp.bfloat16)
        .reshape(latents_here, tokens_here, model_width)
    )
    key_all, value_all = (
        lax.all_gather(key_local, "seq", axis=1, tiled=True),
        lax.all_gather(value_local, "seq", axis=1, tiled=True),
    )
    key_count = key_all.shape[1]
    key_heads = key_all.reshape(latents_here, key_count, head_count, head_size)
    value_heads = value_all.reshape(latents_here, key_count, head_count, head_size)
    scores = (
        jnp.einsum("bqhd,bkhd->bhqk", query, key_heads, preferred_element_type=jnp.float32)
        * score_scale
    )
    peak = jnp.max(scores, axis=-1, keepdims=True)
    log_total = jnp.log(jnp.sum(jnp.exp(scores - peak), axis=-1, keepdims=True)) + peak
    softmaxed = jnp.exp(scores - log_total)
    attended = jnp.einsum(
        "bhqk,bkhd->bqhd",
        softmaxed.astype(jnp.bfloat16),
        value_heads,
        preferred_element_type=jnp.float32,
    )
    attended = attended.astype(jnp.bfloat16).reshape(row_count, model_width)
    attention = (matmul(attended, full_proj) + bias_proj).reshape(
        latents_here, tokens_here, model_width
    )
    middle = inputs + gate_one * attention
    normed_two, norm_pull_two = jax.vjp(normalize, middle)
    second_rows = (
        (normed_two * (1.0 + scale_two) + shift_two)
        .astype(jnp.bfloat16)
        .reshape(row_count, model_width)
    )
    hidden = matmul(second_rows, full_fc1) + bias_fc1
    active, gelu_pull = jax.vjp(gelu_tanh, hidden)
    active_low = active.astype(jnp.bfloat16)
    branch = (matmul(active_low, full_fc2) + bias_fc2).reshape(
        latents_here, tokens_here, model_width
    )
    output = (middle + gate_two * branch).astype(jnp.bfloat16)
    regained = collect_back(w_ada, w_qkv, w_proj, w_fc1, w_fc2)
    full_ada, full_qkv, full_proj, full_fc1, full_fc2 = (
        regained[0],
        regained[1],
        regained[2],
        regained[3],
        regained[4],
    )
    grad_out = cotangent.astype(jnp.float32)
    gate_two_grad = jnp.sum(grad_out * branch, axis=1)
    branch_grad = (gate_two * grad_out).astype(jnp.bfloat16).reshape(row_count, model_width)
    fc2_bias_grad = jnp.sum(branch_grad.astype(jnp.float32), axis=0)
    fc2_grad = contract_rows(active_low, branch_grad)
    active_grad = contract_cols(branch_grad, full_fc2)
    hidden_grad = gelu_pull(active_grad)[0].astype(jnp.bfloat16)
    fc1_bias_grad = jnp.sum(hidden_grad.astype(jnp.float32), axis=0)
    fc1_grad = contract_rows(second_rows, hidden_grad)
    second_grad = contract_cols(hidden_grad, full_fc1).reshape(
        latents_here, tokens_here, model_width
    )
    shift_two_grad = jnp.sum(second_grad, axis=1)
    scale_two_grad = jnp.sum(second_grad * normed_two, axis=1)
    middle_grad = grad_out + norm_pull_two(second_grad * (1.0 + scale_two))[0]
    gate_one_grad = jnp.sum(middle_grad * attention, axis=1)
    attention_grad = (gate_one * middle_grad).astype(jnp.bfloat16).reshape(row_count, model_width)
    proj_bias_grad = jnp.sum(attention_grad.astype(jnp.float32), axis=0)
    proj_grad = contract_rows(attended, attention_grad)
    attended_grad = contract_cols(attention_grad, full_proj).astype(jnp.bfloat16)
    attended_grad = attended_grad.reshape(latents_here, tokens_here, head_count, head_size)
    scores = (
        jnp.einsum("bqhd,bkhd->bhqk", query, key_heads, preferred_element_type=jnp.float32)
        * score_scale
    )
    softmaxed = jnp.exp(scores - log_total)
    weight_grad = jnp.einsum(
        "bqhd,bkhd->bhqk", attended_grad, value_heads, preferred_element_type=jnp.float32
    )
    row_delta = jnp.sum(softmaxed * weight_grad, axis=-1, keepdims=True)
    score_grad = (softmaxed * (weight_grad - row_delta)).astype(jnp.bfloat16)
    query_grad = (
        jnp.einsum("bhqk,bkhd->bqhd", score_grad, key_heads, preferred_element_type=jnp.float32)
        * score_scale
    )
    key_grad = (
        jnp.einsum("bhqk,bqhd->bkhd", score_grad, query, preferred_element_type=jnp.float32)
        * score_scale
    )
    value_grad = jnp.einsum(
        "bhqk,bqhd->bkhd",
        softmaxed.astype(jnp.bfloat16),
        attended_grad,
        preferred_element_type=jnp.float32,
    )
    key_mine, value_mine = (
        lax.psum_scatter(
            key_grad.reshape(latents_here, key_count, model_width).astype(jnp.bfloat16),
            "seq",
            scatter_dimension=1,
            tiled=True,
        ).astype(jnp.float32),
        lax.psum_scatter(
            value_grad.reshape(latents_here, key_count, model_width).astype(jnp.bfloat16),
            "seq",
            scatter_dimension=1,
            tiled=True,
        ).astype(jnp.float32),
    )
    query_low = query_grad.astype(jnp.bfloat16).reshape(row_count, model_width)
    value_low = value_mine.astype(jnp.bfloat16).reshape(row_count, model_width)
    joint_grad = jnp.concatenate(
        [query_low, key_mine.astype(jnp.bfloat16).reshape(row_count, model_width), value_low],
        axis=-1,
    )
    query_bias_grad = jnp.sum(query_low.astype(jnp.float32), axis=0)
    value_bias_grad = jnp.sum(value_low.astype(jnp.float32), axis=0)
    qkv_grad = contract_rows(first_rows, joint_grad)
    first_grad = contract_cols(joint_grad, full_qkv).reshape(latents_here, tokens_here, model_width)
    shift_one_grad = jnp.sum(first_grad, axis=1)
    scale_one_grad = jnp.sum(first_grad * normed_one, axis=1)
    input_grad = middle_grad + norm_pull_one(first_grad * (1.0 + scale_one))[0]
    mods_grad = jnp.concatenate(
        [
            shift_one_grad,
            scale_one_grad,
            gate_one_grad,
            shift_two_grad,
            scale_two_grad,
            gate_two_grad,
        ],
        axis=-1,
    )
    mods_low = lax.psum(mods_grad.astype(jnp.bfloat16), "seq")
    leader = (lax.axis_index("seq") == 0).astype(jnp.float32)
    ada_grad = contract_rows(smooth_low, mods_low) * leader
    ada_bias_grad = jnp.sum(mods_low.astype(jnp.float32), axis=0) * leader
    smooth_grad = contract_cols(mods_low, full_ada)
    condition_grad = silu_pull(smooth_grad)[0]
    summed = (
        lax.psum_scatter(
            ada_grad.astype(jnp.bfloat16), "dp", scatter_dimension=0, tiled=True
        ).astype(jnp.float32),
        lax.psum_scatter(
            qkv_grad.astype(jnp.bfloat16), "dp", scatter_dimension=0, tiled=True
        ).astype(jnp.float32),
        lax.psum_scatter(
            proj_grad.astype(jnp.bfloat16), "dp", scatter_dimension=0, tiled=True
        ).astype(jnp.float32),
        lax.psum_scatter(
            fc1_grad.astype(jnp.bfloat16), "dp", scatter_dimension=0, tiled=True
        ).astype(jnp.float32),
        lax.psum_scatter(
            fc2_grad.astype(jnp.bfloat16), "dp", scatter_dimension=0, tiled=True
        ).astype(jnp.float32),
        lax.psum_scatter(
            ada_bias_grad.astype(jnp.bfloat16), "dp", scatter_dimension=0, tiled=True
        ).astype(jnp.float32),
        lax.psum_scatter(
            query_bias_grad.astype(jnp.bfloat16), "dp", scatter_dimension=0, tiled=True
        ).astype(jnp.float32),
        lax.psum_scatter(
            value_bias_grad.astype(jnp.bfloat16), "dp", scatter_dimension=0, tiled=True
        ).astype(jnp.float32),
        lax.psum_scatter(
            proj_bias_grad.astype(jnp.bfloat16), "dp", scatter_dimension=0, tiled=True
        ).astype(jnp.float32),
        lax.psum_scatter(
            fc1_bias_grad.astype(jnp.bfloat16), "dp", scatter_dimension=0, tiled=True
        ).astype(jnp.float32),
        lax.psum_scatter(
            fc2_bias_grad.astype(jnp.bfloat16), "dp", scatter_dimension=0, tiled=True
        ).astype(jnp.float32),
    )
    owned = (
        lax.psum_scatter(
            summed[0].astype(jnp.bfloat16), "seq", scatter_dimension=1, tiled=True
        ).astype(jnp.float32),
        lax.psum_scatter(
            summed[1].astype(jnp.bfloat16), "seq", scatter_dimension=1, tiled=True
        ).astype(jnp.float32),
        lax.psum_scatter(
            summed[2].astype(jnp.bfloat16), "seq", scatter_dimension=1, tiled=True
        ).astype(jnp.float32),
        lax.psum_scatter(
            summed[3].astype(jnp.bfloat16), "seq", scatter_dimension=1, tiled=True
        ).astype(jnp.float32),
        lax.psum_scatter(
            summed[4].astype(jnp.bfloat16), "seq", scatter_dimension=1, tiled=True
        ).astype(jnp.float32),
        lax.psum_scatter(
            summed[5].astype(jnp.bfloat16), "seq", scatter_dimension=0, tiled=True
        ).astype(jnp.float32),
        lax.psum_scatter(
            summed[6].astype(jnp.bfloat16), "seq", scatter_dimension=0, tiled=True
        ).astype(jnp.float32),
        lax.psum_scatter(
            summed[7].astype(jnp.bfloat16), "seq", scatter_dimension=0, tiled=True
        ).astype(jnp.float32),
        lax.psum_scatter(
            summed[8].astype(jnp.bfloat16), "seq", scatter_dimension=0, tiled=True
        ).astype(jnp.float32),
        lax.psum_scatter(
            summed[9].astype(jnp.bfloat16), "seq", scatter_dimension=0, tiled=True
        ).astype(jnp.float32),
        lax.psum_scatter(
            summed[10].astype(jnp.bfloat16), "seq", scatter_dimension=0, tiled=True
        ).astype(jnp.float32),
    )
    return (
        output,
        input_grad,
        condition_grad,
        owned[0],
        owned[5],
        owned[1],
        owned[6],
        owned[7],
        owned[2],
        owned[8],
        owned[3],
        owned[9],
        owned[4],
        owned[10],
    )


NT = (((1,), (1,)), ((), ()))
NN = (((1,), (0,)), ((), ()))


def product(left, right, dims):
    return lax.dot_general(left, right, dims, preferred_element_type=WIDE)


def flat(ref):
    value = ref[...]
    return value.reshape(value.shape[0] * value.shape[2], value.shape[3])


def attention_kernel(q_ref, k_ref, v_ref, o_ref, e_ref, r_ref, *, size):
    q, k, v = flat(q_ref), flat(k_ref), flat(v_ref)
    count = q.shape[0]
    heads = q.shape[1] // size
    scaled = q.astype(WIDE) * (LOG2E * size**-0.5)
    high = scaled.astype(LOW)
    rest = (scaled - high.astype(WIDE)).astype(LOW)
    v_t = v.astype(WIDE).T.astype(LOW)
    ones = jnp.ones((16, count), LOW)

    def score(head):
        cols = slice(head * size, (head + 1) * size)
        keys = jnp.concatenate([k[:, cols], k[:, cols]], 1)
        queries = jnp.concatenate([high[:, cols], rest[:, cols]], 1)
        return product(keys, queries, NT)

    outs, inverses = [], []

    def finish(head, weights):
        values = jnp.concatenate([v_t[head * size : (head + 1) * size], ones], 0)
        summed = product(values, weights, NN)
        inverse = 1.0 / summed[size : size + 1]
        outs.append(summed[:size] * inverse)
        inverses.append(inverse)

    scores, before = score(0), None
    for head in range(heads):
        ahead = score(head + 1) if head + 1 < heads else None
        peak = jnp.max(scores, axis=0, keepdims=True)
        weights = jnp.exp2(scores - peak).astype(LOW)
        e_ref[0, 0, head] = weights
        if before is not None:
            finish(head - 1, before)
        scores, before = ahead, weights
    finish(heads - 1, before)
    o_ref[...] = jnp.concatenate(outs, 0).T.astype(LOW).reshape(o_ref.shape)
    r_ref[0, 0] = jnp.concatenate(inverses, 0)


def attention_back_kernel(
    q_ref, k_ref, v_ref, o_ref, do_ref, e_ref, r_ref, dq_ref, dk_ref, dv_ref, *, size
):
    q, k, v = flat(q_ref), flat(k_ref), flat(v_ref)
    do, o = flat(do_ref).astype(WIDE), flat(o_ref).astype(WIDE)
    scale = size**-0.5
    inverse = r_ref[0, 0]
    prod_t = (do * o).T
    do_t = do.T
    k_t = (k.astype(WIDE) * scale).T.astype(LOW)
    q_scaled = (q.astype(WIDE) * scale).astype(LOW)
    dqs, dks, dvs = [], [], []
    for head in range(q.shape[1] // size):
        cols = slice(head * size, (head + 1) * size)
        inv = inverse[head : head + 1]
        grad_t = do_t[cols] * inv
        delta = jnp.sum(prod_t[cols], axis=0, keepdims=True) * inv
        weights = e_ref[0, 0, head]
        da = product(v[:, cols], grad_t.astype(LOW), NN)
        ds = weights * (da - delta).astype(LOW)
        dqs.append(product(k_t[cols], ds, NN))
        dks.append(product(ds, q_scaled[:, cols], NN))
        dvs.append(product(weights, grad_t.T.astype(LOW), NN))
    dq_ref[...] = jnp.concatenate(dqs, 0).T.astype(LOW).reshape(dq_ref.shape)
    dk_ref[...] = jnp.concatenate(dks, 1).astype(LOW).reshape(dk_ref.shape)
    dv_ref[...] = jnp.concatenate(dvs, 1).astype(LOW).reshape(dv_ref.shape)


PARAMS = pltpu.CompilerParams(vmem_limit_bytes=56 << 20)


def attention_blocks(half, tokens, width):
    def columns(base):
        return pl.BlockSpec((half, 1, tokens, width), lambda latent, pair: (0, latent, 0, base + pair))

    return columns


def attention_fore(qkv):
    half, latents, tokens, triple = qkv.shape
    model = triple // 3
    size = model // HEADS
    per = 128 // size
    pairs = HEADS // per
    count = half * tokens
    columns = attention_blocks(half, tokens, 128)
    flops = 4 * latents * HEADS * count * count * 128
    return pl.pallas_call(
        functools.partial(attention_kernel, size=size),
        grid=(latents, pairs),
        in_specs=[columns(0), columns(pairs), columns(2 * pairs)],
        out_specs=[
            columns(0),
            pl.BlockSpec((1, 1, per, count, count), lambda latent, pair: (latent, pair, 0, 0, 0)),
            pl.BlockSpec((1, 1, per, count), lambda latent, pair: (latent, pair, 0, 0)),
        ],
        out_shape=[
            jax.ShapeDtypeStruct((half, latents, tokens, model), LOW),
            jax.ShapeDtypeStruct((latents, pairs, per, count, count), LOW),
            jax.ShapeDtypeStruct((latents, pairs, per, count), WIDE),
        ],
        compiler_params=PARAMS,
        cost_estimate=pl.CostEstimate(
            flops=flops, bytes_accessed=90 << 20, transcendentals=latents * HEADS * count * count
        ),
        name="attention_fore",
    )(qkv, qkv, qkv)


def attention_back(qkv, attended, attended_grad, weights, inverse):
    half, latents, tokens, triple = qkv.shape
    model = triple // 3
    size = model // HEADS
    per = 128 // size
    pairs = HEADS // per
    count = half * tokens
    columns = attention_blocks(half, tokens, 128)
    flops = 8 * latents * HEADS * count * count * 128
    grads = jax.ShapeDtypeStruct((half, latents, tokens, model), LOW)
    return pl.pallas_call(
        functools.partial(attention_back_kernel, size=size),
        grid=(latents, pairs),
        in_specs=[
            columns(0),
            columns(pairs),
            columns(2 * pairs),
            columns(0),
            columns(0),
            pl.BlockSpec((1, 1, per, count, count), lambda latent, pair: (latent, pair, 0, 0, 0)),
            pl.BlockSpec((1, 1, per, count), lambda latent, pair: (latent, pair, 0, 0)),
        ],
        out_specs=[columns(0)] * 3,
        out_shape=[grads] * 3,
        compiler_params=PARAMS,
        cost_estimate=pl.CostEstimate(flops=flops, bytes_accessed=100 << 20, transcendentals=0),
        name="attention_back",
    )(qkv, qkv, qkv, attended, attended_grad, weights, inverse)


SIX = 6


def norm_parts(rows):
    centre = rows - jnp.mean(rows, axis=1, keepdims=True)
    inverse = lax.rsqrt(jnp.mean(centre * centre, axis=1, keepdims=True) + 1e-06)
    return centre * inverse, inverse


def norm_back(grad, normed, inverse):
    mean = jnp.mean(grad, axis=1, keepdims=True)
    along = jnp.mean(grad * normed, axis=1, keepdims=True)
    return (grad - mean - normed * along) * inverse


def down_sum(value):
    return jnp.sum(value, axis=0, keepdims=True)


def accumulate(ref, value, start):
    @pl.when(start)
    def _():
        ref[...] = value.reshape(ref.shape)

    @pl.when(jnp.logical_not(start))
    def _():
        ref[...] += value.reshape(ref.shape)


def first_of_latent():
    return (pl.program_id(1) == 0) & (pl.program_id(2) == 0)


def first_of_all():
    return (pl.program_id(0) == 0) & first_of_latent()


class Bundle:
    def __init__(self, ref, hidden):
        self.ref = ref
        self.dp, rows, self.width = ref.shape
        self.count = hidden // self.width
        self.high = self.width // self.dp
        self.low = hidden // self.dp

    def take(self, places, rows):
        return self.ref[places, rows, :].reshape(self.width, self.width)

    def fc1(self, block):
        return self.take(slice(0, self.dp), slice(block * self.high, (block + 1) * self.high))

    def proj(self):
        return self.fc1(self.count)

    def fc2(self, block):
        start = (self.count + 1) * self.high
        per = self.dp // self.count
        return self.take(slice(block * per, (block + 1) * per), slice(start, start + self.low))


def project_kernel(x_ref, mods_ref, w_ref, bias_ref, first_ref, qkv_ref):
    mods = mods_ref[0]
    normed, _ = norm_parts(x_ref[0, 0].astype(WIDE))
    first = (normed * (1.0 + mods[1:2]) + mods[0:1]).astype(LOW)
    first_ref[0, 0] = first
    model = first.shape[1]
    for at in range(0, 3 * model, model):
        cols = slice(at, at + model)
        qkv_ref[0, 0, :, cols] = (product(first, w_ref[:, cols], NN) + bias_ref[:, cols]).astype(LOW)


def forward_kernel(
    x_ref, o_ref, dy_ref, mods_ref, bundle_ref, b_proj_ref, b1_ref, b2_ref,
    out_ref, sent_ref, second_ref, active_ref, slope_ref, attention_ref, middle_ref, dm_ref, gate_ref,
):
    mods = mods_ref[0]
    bundle = Bundle(bundle_ref, b1_ref.shape[1])
    attention = product(o_ref[0, 0], bundle.proj(), NN) + b_proj_ref[...]
    attention_ref[0, 0] = attention.astype(LOW)
    middle = x_ref[0, 0].astype(WIDE) + mods[2:3] * attention
    middle_ref[0, 0] = middle
    normed, _ = norm_parts(middle)
    second = (normed * (1.0 + mods[4:5]) + mods[3:4]).astype(LOW)
    second_ref[0, 0] = second
    branch = b2_ref[...]
    width = second.shape[1]
    for block in range(bundle.count):
        cols = slice(block * width, (block + 1) * width)
        hidden = product(second, bundle.fc1(block), NN) + b1_ref[:, cols]
        square = hidden * hidden
        bend = jnp.tanh(hidden * (0.7978845608028654 + 0.035677408136300125 * square))
        half = 0.5 + 0.5 * bend
        active = (hidden * half).astype(LOW)
        steep = 0.7978845608028654 + 0.10703222440890037 * square
        slope = half + (0.5 * hidden) * (1.0 - bend * bend) * steep
        active_ref[0, 0, :, cols] = active
        slope_ref[0, 0, :, cols] = slope.astype(LOW)
        branch = branch + product(active, bundle.fc2(block), NN)
    out = (middle + mods[5:6] * branch).astype(LOW)
    out_ref[0, 0] = out
    sent_ref[0] = out
    dy = dy_ref[0, 0].astype(WIDE)
    dm_ref[0, 0] = (mods[5:6] * dy).astype(LOW)
    accumulate(gate_ref, down_sum(dy * branch), first_of_latent())


def backward_kernel(
    dy_ref, dm_ref, slope_ref, middle_ref, attention_ref, mods_ref, bundle_ref,
    dh_ref, dmiddle_ref, dattention_ref, do_ref, sums_ref, b1_ref, b2_ref, b_proj_ref,
):
    mods = mods_ref[0]
    dm = dm_ref[0, 0]
    width = dm.shape[1]
    start = first_of_all()
    dsecond = None
    bundle = Bundle(bundle_ref, b1_ref.shape[1])
    for block in range(bundle.count):
        cols = slice(block * width, (block + 1) * width)
        dh = (product(dm, bundle.fc2(block), NT) * slope_ref[0, 0, :, cols].astype(WIDE)).astype(LOW)
        dh_ref[0, 0, :, cols] = dh
        accumulate(b1_ref.at[:, cols], down_sum(dh.astype(WIDE)), start)
        part = product(dh, bundle.fc1(block), NT)
        dsecond = part if dsecond is None else dsecond + part
    normed, inverse = norm_parts(middle_ref[0, 0])
    dmiddle = dy_ref[0, 0].astype(WIDE) + norm_back(dsecond * (1.0 + mods[4:5]), normed, inverse)
    dmiddle_ref[0, 0] = dmiddle
    dattention = (mods[2:3] * dmiddle).astype(LOW)
    dattention_ref[0, 0] = dattention
    do_ref[0, 0] = product(dattention, bundle.proj(), NT).astype(LOW)
    sums = jnp.concatenate(
        [
            down_sum(dmiddle * attention_ref[0, 0].astype(WIDE)),
            down_sum(dsecond),
            down_sum(dsecond * normed),
        ],
        axis=0,
    )
    accumulate(sums_ref, sums, first_of_latent())
    accumulate(b2_ref, down_sum(dm.astype(WIDE)), start)
    accumulate(b_proj_ref, down_sum(dattention.astype(WIDE)), start)


def project_back_kernel(
    dq_ref, dk_ref, dv_ref, x_ref, dmiddle_ref, mods_ref, w_ref, dx_ref, sent_ref, sums_ref, bq_ref, bv_ref
):
    mods = mods_ref[0]
    model = x_ref.shape[3]
    grads = [dq_ref[0, 0], dk_ref[0, 0], dv_ref[0, 0]]
    dfirst = sum(
        product(grad, w_ref[:, i * model : (i + 1) * model], NT) for i, grad in enumerate(grads)
    )
    normed, inverse = norm_parts(x_ref[0, 0].astype(WIDE))
    dx = dmiddle_ref[0, 0] + norm_back(dfirst * (1.0 + mods[1:2]), normed, inverse)
    dx_ref[0, 0] = dx
    sent_ref[0] = dx.astype(LOW)
    sums = jnp.concatenate([down_sum(dfirst), down_sum(dfirst * normed)], axis=0)
    accumulate(sums_ref, sums, first_of_latent())
    start = first_of_all()
    accumulate(bq_ref, down_sum(grads[0].astype(WIDE)), start)
    accumulate(bv_ref, down_sum(grads[2].astype(WIDE)), start)


def row_call(kernel, like, operands, results, flops, name, span):
    half, latents, tokens, _ = like.shape
    span = min(span, tokens)

    def spec(shape, kind):
        if kind == "rows":
            return pl.BlockSpec((1, 1, span, shape[3]), lambda l, h, i: (h, l, i, 0))
        if kind == "latent":
            return pl.BlockSpec((1,) + shape[1:], lambda l, h, i: (l,) + (0,) * (len(shape) - 1))
        if kind == "whole":
            zeros = (0,) * len(shape)
            return pl.BlockSpec(shape, lambda l, h, i: zeros, pipeline_mode=pl.Buffered(1))
        width, index = kind
        return pl.BlockSpec(
            (shape[0], width), lambda l, h, i: (0, index), pipeline_mode=pl.Buffered(1)
        )

    def out_spec(shape, kind):
        if kind == "all":
            return pl.BlockSpec(shape, lambda l, h, i: (0, 0))
        if kind == "second":
            return pl.BlockSpec((1, span, shape[2]), lambda l, h, i: (l, i, 0))
        return spec(shape, kind)

    return pl.pallas_call(
        kernel,
        grid=(latents, half, tokens // span),
        in_specs=[spec(a.shape, kind) for a, kind in operands],
        out_specs=[out_spec(shape, kind) for shape, _, kind in results],
        out_shape=[jax.ShapeDtypeStruct(shape, dtype) for shape, dtype, _ in results],
        compiler_params=PARAMS,
        cost_estimate=pl.CostEstimate(flops=flops, bytes_accessed=64 << 20, transcendentals=0),
        name=name,
    )(*(a for a, _ in operands))


class Wires:
    def __init__(self, dp):
        self.depth = dp // 4
        index = lax.axis_index("dp")
        self.z, self.y, self.core = index // 4, (index // 2) % 2, index % 2
        self.x = lax.axis_index("seq")
        self.places = [(z, y, c) for z in range(self.depth) for y in range(2) for c in range(2)]

    def across(self, value):
        return lax.ppermute(value, "seq", [(0, 1), (1, 0)])

    def dp_step(self, value, move):
        pairs = []
        for z, y, c in self.places:
            to_z, to_y, to_c = move(z, y, c)
            pairs.append(((z * 2 + y) * 2 + c, (to_z * 2 + to_y) * 2 + to_c))
        return lax.ppermute(value, "dp", pairs)

    def distances(self):
        steps, distance = [], self.depth // 2
        while distance:
            steps.append(distance)
            distance //= 2
        return steps

    def bit(self, distance):
        return (self.z // distance) % 2

    def mirror(self, value, distance):
        return self.dp_step(value, lambda z, y, c: (z ^ distance, y, c))

    def beside(self, value):
        return self.dp_step(value, lambda z, y, c: (z, 1 - y, c))

    def twin(self, value):
        return self.dp_step(value, lambda z, y, c: (z, y, 1 - c))


def pick(value, index, axis):
    return lax.dynamic_index_in_dim(value, index, axis, keepdims=False)


def order_two(mine, other, index, axis, fresh=False):
    if fresh:
        mine, other = mine[:, None], other[:, None]
        both = order_two(mine, other, index, 1)
        return both.reshape((-1,) + both.shape[2:])
    return jnp.where(
        index == 0,
        jnp.concatenate([mine, other], axis),
        jnp.concatenate([other, mine], axis),
    )


def gather_small(wires, value):
    held = value[None]
    for distance in wires.distances():
        held = order_two(held, wires.mirror(held, distance), wires.bit(distance), 0, True)
    held = order_two(held, wires.beside(held), wires.y, 0, True)
    held = order_two(held, wires.twin(held), wires.core, 0, True)
    return held


def sum_small(wires, value):
    held = value.reshape((wires.depth, 2, 2) + value.shape[1:])
    held = pick(held, wires.core, 2) + wires.twin(pick(held, 1 - wires.core, 2))
    held = pick(held, wires.y, 1) + wires.beside(pick(held, 1 - wires.y, 1))
    return sum_line(wires, held, 1)


def sum_line(wires, held, nearest):
    distances = [distance for distance in wires.distances() if distance >= nearest]
    held = held.reshape((2,) * len(distances) + held.shape[1:])
    for place, distance in reversed(list(enumerate(distances))):
        bit = wires.bit(distance)
        held = pick(held, bit, place) + wires.mirror(pick(held, 1 - bit, place), distance)
    return held


def add_low(left, right):
    return (left.astype(WIDE) + right.astype(WIDE)).astype(LOW)


def send_columns(wires, whole):
    halves = whole.reshape(whole.shape[0], 2, whole.shape[1] // 2)
    return pick(halves, wires.x, 1), wires.across(pick(halves, 1 - wires.x, 1))


def add_wide(left, right):
    return left.astype(WIDE) + right.astype(WIDE)


def fast_body(
    dp,
    tokens,
    condition,
    w_ada,
    b_ada,
    w_qkv,
    q_bias,
    v_bias,
    w_proj,
    b_proj,
    w_fc1,
    b_fc1,
    w_fc2,
    b_fc2,
    cotangent,
):
    wires = Wires(dp)
    group, tokens_here, model = tokens.shape
    mine = group // 2
    rows = group * tokens_here
    x, z_y_c = wires.x, lax.axis_index("dp")

    def swap(value):
        ours = lax.dynamic_slice_in_dim(value, x * mine, mine, 0)
        theirs = lax.dynamic_slice_in_dim(value, (1 - x) * mine, mine, 0)
        return ours, wires.across(theirs)

    def swap_back(value, theirs):
        return order_two(value[0], theirs.astype(value.dtype), x, 0)

    packed = jnp.concatenate([w_qkv, w_proj, w_fc1], axis=1)
    theirs = wires.across(packed)
    cuts = [w_qkv.shape[1], w_qkv.shape[1] + w_proj.shape[1]]
    own_qkv, own_proj, own_fc1 = (
        order_two(a, b, x, 1) for a, b in zip(jnp.split(packed, cuts, 1), jnp.split(theirs, cuts, 1))
    )
    own_fc2 = order_two(w_fc2, wires.across(w_fc2), x, 1)
    full_qkv = lax.all_gather(own_qkv, "dp", axis=0, tiled=True)
    blocks = jnp.split(own_fc1, own_fc1.shape[1] // model, 1) + [own_proj, own_fc2]
    bundle = lax.all_gather(jnp.concatenate(blocks, axis=0), "dp", axis=0, tiled=False)
    tokens, own_fc2 = lax.optimization_barrier((tokens, own_fc2))
    tokens_mine, tokens_across = swap(tokens)

    vectors = (q_bias, v_bias, b_proj, b_fc1, b_fc2, b_ada)
    sizes = [v.shape[0] for v in vectors]
    offsets = [sum(sizes[:i]) for i in range(len(sizes))]
    biases = jnp.concatenate(vectors)[None]
    biases = order_two(biases, wires.across(biases), x, 0)
    smooth, silu_pull = jax.vjp(jax.nn.silu, condition)
    smooth_low = smooth.astype(LOW)
    vector = jnp.concatenate([smooth_low.reshape(-1), biases.reshape(-1)])
    vector = gather_small(wires, vector)
    joined = vector[:, group * model :].reshape(2 * dp, -1)
    bias_query, bias_value, bias_proj, bias_fc1, bias_fc2, bias_ada = (
        joined[:, o : o + n].reshape(-1).astype(WIDE) for o, n in zip(offsets, sizes)
    )

    smooth_all = vector[:, : group * model].reshape(dp * group, model)
    ada_rows = w_ada.shape[0]
    smooth_mine = lax.dynamic_slice_in_dim(smooth_all, z_y_c * ada_rows, ada_rows, 1)
    partial = matmul(smooth_mine, w_ada)
    half_mods = sum_small(wires, partial.reshape(dp, group, -1))
    tokens_across, half_mods = lax.optimization_barrier((tokens_across, half_mods))
    tokens_two = jnp.stack([tokens_mine, tokens_across])
    ours, theirs = swap(half_mods)
    mods = order_two(ours, theirs, x, 1) + bias_ada
    mods = mods.reshape(mine, SIX, model)
    hidden_width = dp * w_fc2.shape[0]
    rows4 = lambda width: (2, mine, tokens_here, width)
    bias_row = jnp.concatenate([bias_query, jnp.zeros_like(bias_query), bias_value])[None]
    first, qkv = row_call(
        project_kernel,
        tokens_two,
        [
            (tokens_two, "rows"),
            (mods, "latent"),
            (full_qkv, (3 * model, 0)),
            (bias_row, (3 * model, 0)),
        ],
        [(rows4(model), LOW, "rows"), (rows4(3 * model), LOW, "rows")],
        6 * rows * model * model,
        "project",
        512,
    )
    cotangent, w_ada, qkv = lax.optimization_barrier((cotangent, w_ada, qkv))
    ada_across = wires.across(w_ada)
    ours, theirs = swap(cotangent)
    attended, weights, inverse = attention_fore(qkv)
    ada_across, theirs, attended = lax.optimization_barrier((ada_across, theirs, attended))
    both_ada = order_two(w_ada, ada_across, x, 1)
    cotangent_two = jnp.stack([ours, theirs])
    (output, sent, second, active, slope, attention, middle, branch_grad, gate_two_grad) = row_call(
        forward_kernel,
        tokens_two,
        [
            (tokens_two, "rows"),
            (attended, "rows"),
            (cotangent_two, "rows"),
            (mods, "latent"),
            (bundle, "whole"),
            (bias_proj[None], (model, 0)),
            (bias_fc1[None], (hidden_width, 0)),
            (bias_fc2[None], (model, 0)),
        ],
        [
            (rows4(model), LOW, "rows"),
            (rows4(model)[1:], LOW, "second"),
            (rows4(model), LOW, "rows"),
            (rows4(hidden_width), LOW, "rows"),
            (rows4(hidden_width), LOW, "rows"),
            (rows4(model), LOW, "rows"),
            (rows4(model), WIDE, "rows"),
            (rows4(model), LOW, "rows"),
            ((mine, 1, model), WIDE, "latent"),
        ],
        2 * rows * model * (model + 2 * hidden_width),
        "forward",
        256,
    )

    def flat_rows(value):
        return value.reshape(rows, value.shape[-1])

    output_across = wires.across(sent)
    fc2_grad = contract_rows(flat_rows(active), flat_rows(branch_grad)).astype(LOW)
    branch_grad, fc2_grad = lax.optimization_barrier((branch_grad, fc2_grad))
    fc2_rows = lax.psum_scatter(fc2_grad, "dp", scatter_dimension=0, tiled=True)
    (
        hidden_grad,
        middle_grad,
        attention_grad,
        attended_grad,
        middle_sums,
        fc1_bias_grad,
        fc2_bias_grad,
        proj_bias_grad,
    ) = row_call(
        backward_kernel,
        tokens_two,
        [
            (cotangent_two, "rows"),
            (branch_grad, "rows"),
            (slope, "rows"),
            (middle, "rows"),
            (attention, "rows"),
            (mods, "latent"),
            (bundle, "whole"),
        ],
        [
            (rows4(hidden_width), LOW, "rows"),
            (rows4(model), WIDE, "rows"),
            (rows4(model), LOW, "rows"),
            (rows4(model), LOW, "rows"),
            ((mine, 3, model), WIDE, "latent"),
            ((1, hidden_width), WIDE, "all"),
            ((1, model), WIDE, "all"),
            ((1, model), WIDE, "all"),
        ],
        2 * rows * model * (model + 2 * hidden_width),
        "backward",
        256,
    )
    fc1_grad = contract_rows(flat_rows(second), flat_rows(hidden_grad)).astype(LOW)
    attention_grad, fc1_grad = lax.optimization_barrier((attention_grad, fc1_grad))
    fc1_rows = lax.psum_scatter(fc1_grad, "dp", scatter_dimension=0, tiled=True)
    proj_grad = contract_rows(flat_rows(attended), flat_rows(attention_grad)).astype(LOW)
    attended_grad, proj_grad, fc2_rows = lax.optimization_barrier((attended_grad, proj_grad, fc2_rows))
    fc2_kept, fc2_across = send_columns(wires, fc2_rows)
    dq, dk, dv = attention_back(qkv, attended, attended_grad, weights, inverse)
    dq, output_across, fc2_across = lax.optimization_barrier((dq, output_across, fc2_across))
    first_rows = flat_rows(first)
    joint = jnp.concatenate([flat_rows(dq), flat_rows(dk)], axis=-1)
    by_place = (wires.depth, 2, 2, -1, 2 * model)
    left = contract_rows(first_rows, joint).astype(LOW).reshape(by_place)
    left_twins = wires.twin(pick(left, 1 - wires.core, 2))
    left, dv = lax.optimization_barrier((left, dv))
    value_grad = contract_rows(first_rows, flat_rows(dv)).astype(LOW)
    right = jnp.concatenate([value_grad, proj_grad], axis=1).reshape(by_place)
    right_twins = wires.twin(pick(right, 1 - wires.core, 2))
    dk, left_twins, right_twins, fc1_rows = lax.optimization_barrier(
        (dk, left_twins, right_twins, fc1_rows)
    )
    fc1_kept, fc1_across = send_columns(wires, fc1_rows)
    left = add_low(pick(left, wires.core, 2), left_twins)
    right = add_low(pick(right, wires.core, 2), right_twins)
    right = right.reshape((wires.depth // 2, 2) + right.shape[1:])
    low_bit = wires.bit(1)
    left_keep, left_send = pick(left, wires.y, 1), pick(left, 1 - wires.y, 1)
    right_keep, right_send = pick(right, low_bit, 1), pick(right, 1 - low_bit, 1)
    dk, left_send, right_send = lax.optimization_barrier((dk, left_send, right_send))
    left_across, right_across = wires.beside(left_send), wires.mirror(right_send, 1)
    input_grad, sent, first_sums, query_bias_grad, value_bias_grad = row_call(
        project_back_kernel,
        tokens_two,
        [
            (dq, "rows"),
            (dk, "rows"),
            (dv, "rows"),
            (tokens_two, "rows"),
            (middle_grad, "rows"),
            (mods, "latent"),
            (full_qkv, (3 * model, 0)),
        ],
        [
            (rows4(model), WIDE, "rows"),
            (rows4(model)[1:], LOW, "second"),
            ((mine, 2, model), WIDE, "latent"),
            ((1, model), WIDE, "all"),
            ((1, model), WIDE, "all"),
        ],
        6 * rows * model * model,
        "project_back",
        512,
    )
    sent, first_sums, query_bias_grad, value_bias_grad, left_across, right_across, fc1_across = (
        lax.optimization_barrier(
            (sent, first_sums, query_bias_grad, value_bias_grad, left_across, right_across, fc1_across)
        )
    )
    sent, fc2_across, output_across = lax.optimization_barrier((sent, fc2_across, output_across))
    left, right = add_low(left_keep, left_across), add_low(right_keep, right_across)

    mods_grad = jnp.concatenate([first_sums, middle_sums, gate_two_grad], axis=1).astype(LOW)
    mods_grad = mods_grad.reshape(mine, SIX * model)
    sums = (query_bias_grad, value_bias_grad, proj_bias_grad, fc1_bias_grad, fc2_bias_grad)
    bias_sums = jnp.concatenate([v.reshape(2 * dp, -1) for v in sums], axis=1).reshape(dp, 2, -1)
    bias_sums = pick(bias_sums, x, 1) + wires.across(pick(bias_sums, 1 - x, 1))
    group_grad = order_two(mods_grad, wires.across(mods_grad), x, 0)
    sent, group_grad, bias_sums = lax.optimization_barrier((sent, group_grad, bias_sums))
    input_across = wires.across(sent)
    left = sum_line(wires, left, 1)
    right = add_low(pick(right, wires.y, 1), wires.beside(pick(right, 1 - wires.y, 1)))
    right = sum_line(wires, right, 2)
    fc1_grad, fc2_grad = add_wide(fc1_kept, fc1_across), add_wide(fc2_kept, fc2_across)
    output = swap_back(output, output_across)
    left, right, input_across = lax.optimization_barrier((left, right, input_across))
    input_grad = swap_back(input_grad, input_across)
    last_rows = jnp.concatenate([left, right], axis=1)
    qkv_kept, qkv_across = send_columns(wires, last_rows[:, : 3 * model])
    proj_kept, proj_across = send_columns(wires, last_rows[:, 3 * model :])
    qkv_grad, proj_grad = add_wide(qkv_kept, qkv_across), add_wide(proj_kept, proj_across)
    owned = sum_small(wires, bias_sums)
    all_grad = gather_small(wires, group_grad).reshape(dp * group, -1)
    half_grad = lax.dynamic_slice_in_dim(all_grad, x * 3 * model, 3 * model, 1)
    ada_grad = contract_rows(smooth_mine, half_grad)
    ada_bias_grad = lax.dynamic_slice_in_dim(
        jnp.sum(all_grad.astype(WIDE), axis=0), (z_y_c * 2 + x) * b_ada.shape[0], b_ada.shape[0], 0
    )
    smooth_part = contract_cols(all_grad, both_ada)
    spread = lax.all_to_all(
        smooth_part.reshape(dp, group, ada_rows), "dp", 0, 0, tiled=False
    )
    smooth_grad = jnp.swapaxes(spread, 0, 1).reshape(group, model)
    condition_grad = silu_pull(smooth_grad)[0]

    bias_grads = [owned[o : o + n] for o, n in zip(offsets, sizes[:5])]
    return (
        output,
        input_grad,
        condition_grad,
        ada_grad,
        ada_bias_grad,
        qkv_grad,
        bias_grads[0],
        bias_grads[1],
        proj_grad,
        bias_grads[2],
        fc1_grad,
        bias_grads[3],
        fc2_grad,
        bias_grads[4],
    )


def solution(mesh):
    sizes = dict(mesh.shape)

    def body(tokens, *others):
        split = sizes["seq"] == 2 and sizes["dp"] % 4 == 0 and tokens.shape[0] % 2 == 0
        if split:
            return fast_body(sizes["dp"], tokens, *others)
        return general_body(tokens, *others)

    return jax.shard_map(
        body,
        mesh=mesh,
        in_specs=(
            P("dp", "seq", None),
            P("dp", None),
            P("dp", "seq"),
            P(("dp", "seq")),
            P("dp", "seq"),
            P(("dp", "seq")),
            P(("dp", "seq")),
            P("dp", "seq"),
            P(("dp", "seq")),
            P("dp", "seq"),
            P(("dp", "seq")),
            P("dp", "seq"),
            P(("dp", "seq")),
            P("dp", "seq", None),
        ),
        out_specs=(
            P("dp", "seq", None),
            P("dp", "seq", None),
            P("dp", None),
            P("dp", "seq"),
            P(("dp", "seq")),
            P("dp", "seq"),
            P(("dp", "seq")),
            P(("dp", "seq")),
            P("dp", "seq"),
            P(("dp", "seq")),
            P("dp", "seq"),
            P(("dp", "seq")),
            P("dp", "seq"),
            P(("dp", "seq")),
        ),
        check_vma=False,
    )
```
